32 devices in a mesh: req: 8 (over z, y), mp: 4 (over x, core).
Axes of the slice: x: 2, y: 2, z: 4, core: 2. Of those that a mesh axis runs over, the one named last changes fastest.
Arguments:
- hidden_in: bfloat16 [4096, 2048], P(('req', 'mp')), may hold values from -48 to 48
- segment_ids: int32 [8, 512], replicated, may hold values from 0 to 2, never falling along the last dimension, each value on 1 to 256 neighbouring positions
- request_prompt: int32 [256], P('req'), may hold values from 0 to 23, as said below
- page_table: int32 [256, 16], P('req'), may hold values from 0 to 511, as said below
- ln_attn: bfloat16 [2048], replicated, may hold values from 0.5 to 1.5
- w_query: bfloat16 [2048, 2048], P(None, 'mp'), may hold values from -0.125 to 0.125
- w_key: bfloat16 [2048, 1024], P(None, 'mp'), may hold values from -0.125 to 0.125
- w_value: bfloat16 [2048, 1024], P(None, 'mp'), may hold values from -0.125 to 0.125
- q_gain: bfloat16 [128], replicated, may hold values from 0.5 to 1.5
- k_gain: bfloat16 [128], replicated, may hold values from 0.5 to 1.5
- w_out: bfloat16 [2048, 2048], P('mp'), may hold values from -0.125 to 0.125
- ln_mlp: bfloat16 [2048], replicated, may hold values from 0.5 to 1.5
- w_gate: bfloat16 [2048, 3072], P(None, 'mp'), may hold values from -0.125 to 0.125
- w_up: bfloat16 [2048, 3072], P(None, 'mp'), may hold values from -0.125 to 0.125
- w_down: bfloat16 [3072, 2048], P('mp'), may hold values from -0.109375 to 0.109375
Outputs:
- layer_out: bfloat16 [4096, 2048], P(('req', 'mp'))
- kv_pages: bfloat16 [4096, 16, 8, 256], P('req', None, 'mp')
The draws below stay inside these ranges and needn't reach their ends.
Inputs may be any that keep to these rules, and one draw needn't show every extreme that they name: `request_prompt`: every prompt is continued by 8 to 16 requests, and some prompt by exactly 16. `page_table`: the 32 rows of one index of req name each of the 512 pages once.
All inputs are finite; a program needn't handle non-finite values.
Results may differ from the reference program's by a relative error of at most 0.0075.
Values may be sent and summed in bfloat16 or wider, within the bound.
No kernel may reach another device: no remote copies, remote signals or barrier semaphores. Data moves between devices by JAX's collectives and lax.ppermute only.
A program may use at most 128 MiB of HBM per device.

```python
import math
import jax
import jax.numpy as jnp
import numpy as np
from jax import lax

D = 2048
H = 16
KVH = 8
HD = 128
FF = 3072
SEQ_ROWS = 512
PROMPTS_DEV = 3
REQ_DEV = 32
PAGE = 16
PROMPT_MAX = 256
MAXP = 16
PAGES_DEV = 512
TOKENS = 4096
PROMPTS = 24
REQS = 256
N_REQ = 8


def draw_hidden_in(key, part):
    base_key, row_key, column_key = jax.random.split(key, 3)
    row_scale = jnp.exp(jax.random.uniform(row_key, (TOKENS, 1), jnp.float32, jnp.log(0.4), jnp.log(4.0)))
    column_scale = jnp.exp(jax.random.uniform(column_key, (1, D), jnp.float32, jnp.log(0.3), jnp.log(3.0)))
    base = jax.random.normal(base_key, (TOKENS, D), jnp.float32)
    base = jnp.clip(base, -4.0, 4.0)
    return (base * row_scale * column_scale).astype(jnp.bfloat16)


def draw_request_prompt(key, part):
    spread_key, label_key, order_key = jax.random.split(key, 3)
    base = jnp.repeat(jnp.arange(PROMPTS, dtype=jnp.int32), 8)
    others = jax.random.permutation(spread_key, jnp.repeat(jnp.arange(1, PROMPTS, dtype=jnp.int32), 8))
    extra = jnp.concatenate([jnp.zeros((8,), jnp.int32), others])[:REQS - 8 * PROMPTS]
    relabel = jax.random.permutation(label_key, PROMPTS).astype(jnp.int32)
    every = relabel[jnp.concatenate([base, extra])]
    return jax.random.permutation(order_key, every).astype(jnp.int32)


def draw_page_table(key, part):
    keys = jax.random.split(key, REQS // REQ_DEV)
    tables = jax.vmap(lambda single: jax.random.permutation(single, PAGES_DEV))(keys)
    return tables.astype(jnp.int32).reshape(REQS, MAXP)


def levels(key, shape, shards, low, top_value):
    def one(dim, parts):
        steps = jax.random.uniform(jax.random.fold_in(jax.random.fold_in(key, 6), dim), (parts,), jnp.float32, low / len(shards), top_value / len(shards))
        return jnp.repeat(jnp.exp(steps), shape[dim] // parts).reshape((-1,) + (1,) * (len(shape) - dim - 1))

    level = one(*shards[0])
    for cut in shards[1:]:
        level = level * one(*cut)
    return level


def length_profile(number_of, total, limit, skew):
    loads = [(1 << 20) // math.isqrt(rank ** skew) + 1 for rank in range(2, number_of + 1)]
    rest, given = total - limit - (number_of - 1), [1] * (number_of - 1)
    while rest > 0:
        candidates = [i for i in range(number_of - 1) if given[i] < limit]
        whole, remaining = sum([loads[i] for i in candidates]), rest
        for i in candidates:
            more = min(limit - given[i], max(1, remaining * loads[i] // whole), rest)
            given[i] = given[i] + more
            rest = rest - more
    return np.array([limit] + given)


def ragged_sizes(rng, amount, total, most, lean):
    if amount == 2:
        one = jax.random.randint(rng, (), max(1, total - most), min(most, total - 1) + 1)
        return jnp.stack([one, total - one])
    sizes = jnp.asarray(length_profile(amount, total, most, lean), jnp.int32)
    pairs = (amount - 1) // 2
    giver, taker = sizes[1:1 + 2 * pairs:2], sizes[2:2 + 2 * pairs:2]
    slack = jnp.minimum(giver - 1, most - taker)
    shifted = jax.random.randint(jax.random.fold_in(rng, 1), (pairs,), 0, 1 << 20) % (slack + 1)
    sizes = sizes.at[1:1 + 2 * pairs:2].set(giver - shifted).at[2:2 + 2 * pairs:2].set(taker + shifted)
    return sizes[jax.random.permutation(jax.random.fold_in(rng, 2), amount)]


def normal_values(key, shape, deviation, reach, pieces=(), held_as=jnp.bfloat16):
    entries = deviation * jax.random.normal(key, shape, jnp.float32)
    if pieces:
        entries = entries * levels(key, shape, pieces, -0.22, 0.18)
    return jnp.clip(entries, -reach, reach).astype(held_as)


def setup_inputs(seed: int = 0) -> dict:
    key_list = jax.random.split(jax.random.key(seed), 16)
    return {
        "hidden_in": draw_hidden_in(jax.random.fold_in(key_list[15], 71), 0),
        "segment_ids": jax.vmap(lambda own: jnp.searchsorted(jnp.cumsum(ragged_sizes(own, PROMPTS_DEV, SEQ_ROWS, PROMPT_MAX, 1)), jnp.arange(SEQ_ROWS), side="right"))(jax.random.split(key_list[1], N_REQ)).reshape((N_REQ, SEQ_ROWS)).astype(jnp.int32),
        "request_prompt": draw_request_prompt(jax.random.fold_in(key_list[15], 71), 0),
        "page_table": draw_page_table(jax.random.fold_in(key_list[15], 71), 0),
        "ln_attn": jnp.clip(1.0 + 0.1 * jax.random.normal(key_list[4], (D,), jnp.float32), 0.5, 1.5).astype(jnp.bfloat16),
        "w_query": normal_values(key_list[5], (D, H * HD), D ** -0.5, 0.125, ((1, 4),)),
        "w_key": normal_values(key_list[6], (D, KVH * HD), D ** -0.5, 0.125, ((1, 4),)),
        "w_value": normal_values(key_list[7], (D, KVH * HD), D ** -0.5, 0.125, ((1, 4),)),
        "q_gain": jnp.clip(1.0 + 0.1 * jax.random.normal(key_list[8], (HD,), jnp.float32), 0.5, 1.5).astype(jnp.bfloat16),
        "k_gain": jnp.clip(1.0 + 0.1 * jax.random.normal(key_list[9], (HD,), jnp.float32), 0.5, 1.5).astype(jnp.bfloat16),
        "w_out": normal_values(key_list[10], (H * HD, D), (H * HD) ** -0.5, 0.125, ((0, 4),)),
        "ln_mlp": jnp.clip(1.0 + 0.1 * jax.random.normal(key_list[11], (D,), jnp.float32), 0.5, 1.5).astype(jnp.bfloat16),
        "w_gate": normal_values(key_list[12], (D, FF), D ** -0.5, 0.125, ((1, 4),)),
        "w_up": normal_values(key_list[13], (D, FF), D ** -0.5, 0.125, ((1, 4),)),
        "w_down": normal_values(key_list[14], (FF, D), FF ** -0.5, 0.109375, ((0, 4),)),
    }


EPS = 1e-06
THETA = 1000000.0

def rms_scale(values, gain):
    wide = values.astype(jnp.float32)
    return wide * lax.rsqrt(lax.optimization_barrier(jnp.mean(wide * wide, axis=-1, keepdims=True)) + EPS) * gain.astype(jnp.float32)

def segment_table(segment_row):
    member = (segment_row[:, None] == jnp.arange(PROMPTS_DEV, dtype=jnp.int32)[None, :]).astype(jnp.int32)
    lengths = lax.optimization_barrier(jnp.sum(member, axis=0)).astype(jnp.int32)
    starts = (jnp.cumsum(lengths) - lengths).astype(jnp.int32)
    index = jnp.arange(segment_row.shape[0], dtype=jnp.int32)
    position = (index - lax.optimization_barrier(jnp.sum(member * starts[None, :], axis=1))).astype(jnp.int32)
    return (starts, lengths, position)

def rotate(values, position):
    half = HD // 2
    freq = THETA ** (-(jnp.arange(half, dtype=jnp.float32) * 2.0) / HD)
    angle = position.astype(jnp.float32)[:, None] * freq[None, :]
    cosine = jnp.cos(angle)[:, None, :]
    sine = jnp.sin(angle)[:, None, :]
    first = values[..., :half]
    second = values[..., half:]
    return jnp.concatenate([first * cosine - second * sine, second * cosine + first * sine], axis=-1)

def reference(hidden_in, segment_ids, request_prompt, page_table, ln_attn, w_query, w_key, w_value, q_gain, k_gain, w_out, ln_mlp, w_gate, w_up, w_down):
    group = H // KVH

    def layer_group(inputs):
        rows, segment_row = inputs
        count = rows.shape[0]
        unused_starts, unused_lengths, position = segment_table(segment_row)
        normed = rms_scale(rows, ln_attn).astype(jnp.bfloat16)
        query = jnp.dot(normed, w_query, preferred_element_type=jnp.float32).reshape(count, H, HD)
        key = jnp.dot(normed, w_key, preferred_element_type=jnp.float32).reshape(count, KVH, HD)
        value = jnp.dot(normed, w_value, preferred_element_type=jnp.float32).astype(jnp.bfloat16).reshape(count, KVH, HD)
        query = rotate(rms_scale(query, q_gain), position).astype(jnp.bfloat16)
        key = rotate(rms_scale(key, k_gain), position).astype(jnp.bfloat16)
        grouped = query.reshape(count, KVH, group, HD).astype(jnp.float32)
        scores = jnp.einsum('qcgd,kcd->cgqk', grouped, key.astype(jnp.float32)) / math.sqrt(HD)
        index = jnp.arange(count, dtype=jnp.int32)
        allowed = (segment_row[:, None] == segment_row[None, :]) & (index[None, :] <= index[:, None])
        raised = jnp.where(allowed[None, None], jnp.exp(scores), 0.0)
        weights = (raised / lax.optimization_barrier(jnp.sum(raised, axis=-1, keepdims=True))).astype(jnp.bfloat16)
        mixed = jnp.einsum('cgqk,kcd->qcgd', weights.astype(jnp.float32), value.astype(jnp.float32))
        attended = mixed.reshape(count, H * HD).astype(jnp.bfloat16)
        after = (rows.astype(jnp.float32) + jnp.dot(attended, w_out, preferred_element_type=jnp.float32)).astype(jnp.bfloat16)
        normed_mlp = rms_scale(after, ln_mlp).astype(jnp.bfloat16)
        gate = jnp.dot(normed_mlp, w_gate, preferred_element_type=jnp.float32)
        upper = jnp.dot(normed_mlp, w_up, preferred_element_type=jnp.float32)
        hidden = (jax.nn.silu(gate) * upper).astype(jnp.bfloat16)
        result = (after.astype(jnp.float32) + jnp.dot(hidden, w_down, preferred_element_type=jnp.float32)).astype(jnp.bfloat16)
        pairs = jnp.concatenate([key, value], axis=-1)
        return (result, pairs)
    blocks = hidden_in.reshape(N_REQ, SEQ_ROWS, D)
    results, pairs = lax.map(layer_group, (blocks, segment_ids))
    pairs_flat = pairs.reshape(N_REQ * SEQ_ROWS, KVH, 2 * HD)
    all_starts, all_lengths, unused = jax.vmap(segment_table)(segment_ids)
    flat_starts = all_starts.reshape(-1)
    flat_lengths = all_lengths.reshape(-1)

    def fill_pool(inputs):
        table_block, prompt_block = inputs
        owner = jnp.zeros((PAGES_DEV,), jnp.int32).at[table_block.reshape(-1)].set(jnp.arange(PAGES_DEV, dtype=jnp.int32))
        request = owner // MAXP
        page = owner % MAXP
        prompt = prompt_block[request]
        begin = prompt // PROMPTS_DEV * SEQ_ROWS + flat_starts[prompt]
        length = flat_lengths[prompt]
        offset = page[:, None] * PAGE + jnp.arange(PAGE, dtype=jnp.int32)[None, :]
        valid = offset < length[:, None]
        source = jnp.where(valid, begin[:, None] + offset, 0).astype(jnp.int32)
        taken = pairs_flat[source]
        return jnp.where(valid[:, :, None, None], taken, jnp.zeros((), jnp.bfloat16))
    pools = lax.map(fill_pool, (page_table.reshape(N_REQ, REQ_DEV, MAXP), request_prompt.reshape(N_REQ, REQ_DEV)))
    return (results.reshape(TOKENS, D), pools.reshape(N_REQ * PAGES_DEV, PAGE, KVH, 2 * HD))
```

```python
import functools
import math

import jax
import jax.numpy as jnp
from jax import lax
from jax.experimental import pallas as pl
from jax.experimental.pallas import tpu as pltpu
from jax.sharding import PartitionSpec as P

HD = 128
PROMPTS_DEV = 3
PAGE = 16


EPS = 1e-06
THETA = 1000000.0


def rms_scale(values, gain):
    wide = values.astype(jnp.float32)
    return (
        wide
        * lax.rsqrt(jnp.mean(wide * wide, axis=-1, keepdims=True) + EPS)
        * gain.astype(jnp.float32)
    )


def segment_table(segment_row):
    member = (segment_row[:, None] == jnp.arange(PROMPTS_DEV, dtype=jnp.int32)[None, :]).astype(
        jnp.int32
    )
    lengths = jnp.sum(member, axis=0)
    starts = jnp.cumsum(lengths) - lengths
    index = jnp.arange(segment_row.shape[0], dtype=jnp.int32)
    position = index - jnp.sum(member * starts[None, :], axis=1)
    return (starts, lengths, position)


def rotate(values, position):
    half = HD // 2
    freq = THETA ** (-(jnp.arange(half, dtype=jnp.float32) * 2.0) / HD)
    angle = position.astype(jnp.float32)[:, None] * freq[None, :]
    cosine = jnp.cos(angle)[:, None, :]
    sine = jnp.sin(angle)[:, None, :]
    first = values[..., :half]
    second = values[..., half:]
    return jnp.concatenate(
        [first * cosine - second * sine, second * cosine + first * sine], axis=-1
    )


def segment_bounds(segment_ids):
    limits = jnp.arange(PROMPTS_DEV + 1, dtype=jnp.int32)
    below = segment_ids[:, None, :] < limits[None, :, None]
    return jnp.sum(below.astype(jnp.int32), axis=2).reshape(-1)


def page_kernel(rows, requests, entries, bounds, prompts, table, source, out, blank, sems):
    blank[...] = jnp.zeros_like(blank)

    def pieces(amount, first, start):
        for size in (8, 4, 2, 1):
            skipped = amount - amount % (2 * size)

            @pl.when((amount // size) % 2 == 1)
            def _():
                start(first + skipped, size)

    def issue(r, carry):
        prompt = prompts[r]
        g = prompt // PROMPTS_DEV
        slot = g * (PROMPTS_DEV + 1) + prompt - g * PROMPTS_DEV
        begin = bounds[slot]
        length = bounds[slot + 1] - begin
        begin = g * rows + begin
        full = length // PAGE
        rest = length - full * PAGE

        def copy_page(e, c):
            pltpu.make_async_copy(
                source.at[pl.ds(begin + e * PAGE, PAGE)], out.at[table[r, e]], sems.at[r]
            ).start()
            return c

        lax.fori_loop(0, full, copy_page, 0)

        @pl.when(rest > 0)
        def _():
            page = table[r, full]
            base = begin + full * PAGE

            def kept(at, size):
                pltpu.make_async_copy(
                    source.at[pl.ds(base + at, size)], out.at[page, pl.ds(at, size)], sems.at[r]
                ).start()

            def blanked(at, size):
                pltpu.make_async_copy(
                    blank.at[pl.ds(0, size)], out.at[page, pl.ds(at, size)], sems.at[r]
                ).start()

            pieces(rest, 0, kept)
            pieces(PAGE - rest, rest, blanked)

        def clear_page(e, c):
            pltpu.make_async_copy(blank, out.at[table[r, e]], sems.at[r]).start()
            return c

        lax.fori_loop((length + PAGE - 1) // PAGE, entries, clear_page, 0)
        return carry

    lax.fori_loop(0, requests, issue, 0)

    def finish(r, carry):
        pltpu.make_async_copy(
            out.at[pl.ds(0, entries)], out.at[pl.ds(0, entries)], sems.at[r]
        ).wait()
        return carry

    lax.fori_loop(0, requests, finish, 0)


def fill_pages(bounds, request_prompt, page_table, everything, rows):
    requests, entries = page_table.shape
    row_shape = everything.shape[1:]
    scalars = pl.BlockSpec(memory_space=pltpu.SMEM)
    return pl.pallas_call(
        functools.partial(page_kernel, rows, requests, entries),
        out_shape=jax.ShapeDtypeStruct(
            (requests * entries, PAGE) + row_shape, everything.dtype
        ),
        in_specs=[scalars, scalars, scalars, pl.BlockSpec(memory_space=pltpu.VMEM)],
        out_specs=pl.BlockSpec(memory_space=pl.ANY),
        scratch_shapes=[
            pltpu.VMEM((PAGE,) + row_shape, everything.dtype),
            pltpu.SemaphoreType.DMA((requests,)),
        ],
        compiler_params=pltpu.CompilerParams(
            vmem_limit_bytes=everything.size * 2 + (8 << 20)
        ),
        name="fill_pages",
    )(bounds, request_prompt, page_table, everything)


def body(
    hidden_in,
    segment_ids,
    request_prompt,
    page_table,
    ln_attn,
    w_query,
    w_key,
    w_value,
    q_gain,
    k_gain,
    w_out,
    ln_mlp,
    w_gate,
    w_up,
    w_down,
):
    parts = lax.axis_size("mp")
    owner_rows = hidden_in.shape[0]
    seq_rows = owner_rows * parts
    heads_here = w_query.shape[1] // HD
    kv_here = w_key.shape[1] // HD
    group = heads_here // kv_here
    group_index = lax.axis_index("req")
    segment_row = lax.dynamic_index_in_dim(segment_ids, group_index, 0, keepdims=False)
    unused_starts, unused_lengths, position = segment_table(segment_row)
    piece = lax.all_gather(hidden_in, "mp", axis=0, tiled=True)
    count = piece.shape[0]
    normed = rms_scale(piece, ln_attn).astype(jnp.bfloat16)
    query = jnp.dot(normed, w_query, preferred_element_type=jnp.float32).reshape(
        count, heads_here, HD
    )
    project_key = jnp.dot(normed, w_key, preferred_element_type=jnp.float32).reshape(
        count, kv_here, HD
    )
    project_value = jnp.dot(normed, w_value, preferred_element_type=jnp.float32).astype(
        jnp.bfloat16
    )
    query = (
        rotate(rms_scale(query, q_gain), position)
        .astype(jnp.bfloat16)
        .reshape(count, heads_here * HD)
    )
    project_key = (
        rotate(rms_scale(project_key, k_gain), position)
        .astype(jnp.bfloat16)
        .reshape(count, kv_here * HD)
    )
    joined = [query, project_key, project_value]
    projected = jnp.concatenate(joined, axis=1)
    query_width = heads_here * HD
    key_width = kv_here * HD
    query = projected[:, :query_width].reshape(seq_rows, kv_here, group, HD)
    key = projected[:, query_width : query_width + key_width].reshape(seq_rows, kv_here, HD)
    value = projected[:, query_width + key_width : query_width + 2 * key_width].reshape(
        seq_rows, kv_here, HD
    )
    block = min(512, seq_rows)
    blocks = seq_rows // block
    key_index = jnp.arange(seq_rows, dtype=jnp.int32)

    def attend_block(inputs):
        query_block, first = inputs
        scores = jnp.einsum(
            "qcgd,kcd->cgqk", query_block, key, preferred_element_type=jnp.float32
        ) / math.sqrt(HD)
        row_index = first + jnp.arange(block, dtype=jnp.int32)
        allowed = (segment_row[:, None] == segment_row[None, :]) & (
            key_index[None, :] <= row_index[:, None]
        )
        raised = jnp.where(allowed[None, None], jnp.exp(scores), 0.0)
        weights = (raised / jnp.sum(raised, axis=-1, keepdims=True)).astype(jnp.bfloat16)
        mixed = jnp.einsum("cgqk,kcd->qcgd", weights, value, preferred_element_type=jnp.float32)
        return mixed.astype(jnp.bfloat16).reshape(block, query_width)

    attended = lax.map(
        attend_block,
        (
            query.reshape(blocks, block, kv_here, group, HD),
            jnp.arange(blocks, dtype=jnp.int32) * block,
        ),
    )
    attended = attended.reshape(seq_rows, query_width)
    own_sum = lax.psum_scatter(
        jnp.dot(attended, w_out, preferred_element_type=jnp.float32).astype(jnp.bfloat16),
        "mp",
        scatter_dimension=0,
        tiled=True,
    ).astype(jnp.float32)
    after = (hidden_in.astype(jnp.float32) + own_sum).astype(jnp.bfloat16)
    normed_mlp = rms_scale(lax.all_gather(after, "mp", axis=0, tiled=True), ln_mlp).astype(
        jnp.bfloat16
    )
    gate = jnp.dot(normed_mlp, w_gate, preferred_element_type=jnp.float32)
    upper = jnp.dot(normed_mlp, w_up, preferred_element_type=jnp.float32)
    hidden = (jax.nn.silu(gate) * upper).astype(jnp.bfloat16)
    result = (
        after.astype(jnp.float32)
        + lax.psum_scatter(
            jnp.dot(hidden, w_down, preferred_element_type=jnp.float32).astype(jnp.bfloat16),
            "mp",
            scatter_dimension=0,
            tiled=True,
        ).astype(jnp.float32)
    ).astype(jnp.bfloat16)
    pairs = jnp.concatenate([key, value], axis=-1)
    everything = lax.all_gather(pairs, "req", axis=0, tiled=True)
    cache = fill_pages(segment_bounds(segment_ids), request_prompt, page_table, everything, seq_rows)
    return (result, cache)


def solution(mesh):
    return jax.shard_map(
        body,
        mesh=mesh,
        in_specs=(
            P(("req", "mp"), None),
            P(),
            P("req"),
            P("req", None),
            P(),
            P(None, "mp"),
            P(None, "mp"),
            P(None, "mp"),
            P(),
            P(),
            P("mp", None),
            P(),
            P(None, "mp"),
            P(None, "mp"),
            P("mp", None),
        ),
        out_specs=(P(("req", "mp"), None), P("req", None, "mp", None)),
        check_vma=False,
    )
```

```python
import functools
import math

import jax
import jax.numpy as jnp
from jax import lax
from jax.experimental import pallas as pl
from jax.experimental.pallas import tpu as pltpu
from jax.sharding import PartitionSpec as P

HD = 128
PROMPTS_DEV = 3
PAGE = 16
EPS = 1e-06
THETA = 1000000.0
SMEM = pl.BlockSpec(memory_space=pltpu.SMEM)
VMEM = pl.BlockSpec(memory_space=pltpu.VMEM)
ANY = pl.BlockSpec(memory_space=pl.ANY)


def dot(a, b):
    return jnp.dot(a, b, preferred_element_type=jnp.float32)


def normalized(wide, gain):
    return wide * lax.rsqrt(jnp.mean(wide * wide, axis=-1, keepdims=True) + EPS) * gain


def segment_bounds(segment_ids):
    limits = jnp.arange(PROMPTS_DEV + 1, dtype=jnp.int32)
    below = segment_ids[:, None, :] < limits[None, :, None]
    return jnp.sum(below.astype(jnp.int32), axis=2).reshape(-1)


def rotation(bounds, req, first, rows):
    own = lax.dynamic_slice_in_dim(bounds, req * (PROMPTS_DEV + 1), PROMPTS_DEV, 0)
    token = (lax.iota(jnp.int32, rows) + first) % rows
    start = jnp.max(jnp.where(token[:, None] >= own[None, :], own[None, :], 0), axis=1)
    half = HD // 2
    freq = THETA ** (-(jnp.arange(half, dtype=jnp.float32) * 2.0) / HD)
    angle = (token - start).astype(jnp.float32)[:, None] * freq[None, :]
    cosine, sine = jnp.cos(angle), jnp.sin(angle)
    return (
        jnp.concatenate([cosine, cosine], axis=1),
        jnp.concatenate([-sine, sine], axis=1),
    )


def project_kernel(place, own, other, ln, wq, wk, wv, qg, kg, cos, sin, q, k, v, pairs, normed):
    core = place[2]
    count = own.shape[0]
    gain = ln[...].astype(jnp.float32)
    for ref, at in ((own, core * count), (other, (1 - core) * count)):
        normed[pl.ds(pl.multiple_of(at, count), count), :] = normalized(
            ref[...].astype(jnp.float32), gain
        ).astype(jnp.bfloat16)
    rows = normed[...]
    cosine, sine = cos[...], sin[...]

    def heads(weight, gain_ref, out):
        wide = dot(rows, weight[...])
        gain = gain_ref[...].astype(jnp.float32)
        for h in range(weight.shape[1] // HD):
            one = normalized(wide[:, h * HD : (h + 1) * HD], gain)
            turned = one * cosine + pltpu.roll(one, HD // 2, 1) * sine
            out[:, h * HD : (h + 1) * HD] = turned.astype(jnp.bfloat16)

    heads(wk, kg, k)
    v[...] = dot(rows, wv[...]).astype(jnp.bfloat16)
    shape = (rows.shape[0], k.shape[1] // HD, HD)
    pairs[...] = jnp.concatenate([k[...].reshape(shape), v[...].reshape(shape)], axis=-1)
    heads(wq, qg, q)


def project(place, own, other, ln, wq, wk, wv, qg, kg, cos, sin, chunk):
    count, width = 2 * own.shape[0], own.shape[1]
    kv_here = wk.shape[1] // HD
    bf = jnp.bfloat16
    table = pl.BlockSpec((count, HD), lambda i: (chunk, 0))

    def full(a):
        return pl.BlockSpec(a.shape, lambda i: (0,) * a.ndim, pipeline_mode=pl.Buffered(1))

    outs = [
        jax.ShapeDtypeStruct((count, wq.shape[1]), bf),
        jax.ShapeDtypeStruct((count, wk.shape[1]), bf),
        jax.ShapeDtypeStruct((count, wv.shape[1]), bf),
        jax.ShapeDtypeStruct((count, kv_here, 2 * HD), bf),
    ]
    return pl.pallas_call(
        project_kernel,
        grid=(1,),
        out_shape=outs,
        in_specs=[SMEM] + [full(a) for a in (own, other, ln, wq, wk, wv, qg, kg)] + [table, table],
        out_specs=[full(o) for o in outs],
        scratch_shapes=[pltpu.VMEM((count, width), bf)],
        compiler_params=pltpu.CompilerParams(vmem_limit_bytes=24 << 20),
        cost_estimate=pl.CostEstimate(
            flops=2 * count * width * (wq.shape[1] + 2 * wk.shape[1]),
            bytes_accessed=8 << 20,
            transcendentals=0,
        ),
        name="project",
    )(place, own, other, ln, wq, wk, wv, qg, kg, cos, sin)


def attend_kernel(place, bounds, qa, qb, ka, kb, va, vb, keep_a, send_a, keep_b, send_b):
    req, side, core = place[0], place[1], place[2]
    half = qa.shape[0]
    count = half // 2
    rows = 2 * half
    kv_here = ka.shape[1] // HD
    group = qa.shape[1] // ka.shape[1]
    slot = req * (PROMPTS_DEV + 1)
    scale = 1.0 / math.sqrt(HD)
    first_a = side * half
    first_b = rows - half - first_a
    column = lax.broadcasted_iota(jnp.int32, (count, half), 1)
    line = lax.broadcasted_iota(jnp.int32, (count, half), 0)
    for q, out, first, part in (
        (qb, send_b, first_b, 1 - core),
        (qb, keep_b, first_b, core),
        (qa, send_a, first_a, 1 - core),
        (qa, keep_a, first_a, core),
    ):
        at = pl.multiple_of(part * count, count)
        token = first + at + line
        start = jnp.zeros_like(token)
        for s in range(1, PROMPTS_DEV):
            begin = bounds[slot + s]
            start = jnp.where(token >= begin, begin, start)
        allowed = [
            (column + base <= token) & (column + base >= start) for base in (first_a, first_b)
        ]
        for j in range(kv_here):
            lanes = slice(j * HD, (j + 1) * HD)
            for h in range(j * group, (j + 1) * group):
                one = q[pl.ds(at, count), h * HD : (h + 1) * HD]
                raised = []
                for keys, mask in zip((ka, kb), allowed):
                    scores = lax.dot_general(
                        one,
                        keys[:, lanes],
                        (((1,), (1,)), ((), ())),
                        preferred_element_type=jnp.float32,
                    )
                    raised.append(jnp.where(mask, jnp.exp(scores * scale), 0.0))
                total = sum(jnp.sum(r, axis=-1, keepdims=True) for r in raised)
                share = 1.0 / total
                mixed = sum(
                    dot((r * share).astype(jnp.bfloat16), values[:, lanes])
                    for r, values in zip(raised, (va, vb))
                )
                out[:, h * HD : (h + 1) * HD] = mixed.astype(jnp.bfloat16)


def attend(place, bounds, qa, qb, ka, kb, va, vb):
    count, width = qa.shape[0] // 2, qa.shape[1]
    out = jax.ShapeDtypeStruct((count, width), jnp.bfloat16)
    return pl.pallas_call(
        attend_kernel,
        out_shape=[out] * 4,
        in_specs=[SMEM, SMEM] + [VMEM] * 6,
        out_specs=[VMEM] * 4,
        compiler_params=pltpu.CompilerParams(vmem_limit_bytes=24 << 20),
        cost_estimate=pl.CostEstimate(
            flops=64 * count * count * width, bytes_accessed=4 << 20, transcendentals=1 << 20
        ),
        name="attend",
    )(place, bounds, qa, qb, ka, kb, va, vb)


def mlp_kernel(first, second, ln, wg, wu, keep, send, normed):
    count = first.shape[0]

    @pl.when(pl.program_id(0) == 0)
    def _():
        gain = ln[...].astype(jnp.float32)
        for ref, at in ((first, 0), (second, count)):
            normed[at : at + count, :] = normalized(
                ref[...].astype(jnp.float32), gain
            ).astype(jnp.bfloat16)

    rows = normed[...]
    gate = dot(rows, wg[...])
    upper = dot(rows, wu[...])
    hidden = (gate / (1.0 + jnp.exp(-gate)) * upper).astype(jnp.bfloat16)
    keep[...] = hidden[:count]
    send[...] = hidden[count:]


def mlp(first, second, ln, wg, wu):
    count, width = first.shape
    units = wg.shape[1]
    step = 256
    whole = pl.BlockSpec((count, width), lambda i: (0, 0), pipeline_mode=pl.Buffered(1))
    weight = pl.BlockSpec((width, step), lambda i: (0, i))
    out = jax.ShapeDtypeStruct((count, units), jnp.bfloat16)
    return pl.pallas_call(
        mlp_kernel,
        grid=(units // step,),
        out_shape=[out] * 2,
        in_specs=[whole, whole, pl.BlockSpec((1, width), lambda i: (0, 0)), weight, weight],
        out_specs=[pl.BlockSpec((count, step), lambda i: (0, i))] * 2,
        scratch_shapes=[pltpu.VMEM((2 * count, width), jnp.bfloat16)],
        compiler_params=pltpu.CompilerParams(vmem_limit_bytes=24 << 20),
        cost_estimate=pl.CostEstimate(
            flops=8 * count * width * units, bytes_accessed=8 << 20, transcendentals=1 << 18
        ),
        name="gate_up",
    )(first, second, ln, wg, wu)


def page_kernel(rows, requests, entries, blocks, *refs):
    place, bounds, prompts, table = refs[:4]
    arrived = refs[4 : 4 + blocks]
    out, held, blank, load_sems, sems = refs[4 + blocks :]
    half = rows // 2
    for i in range(blocks):
        pltpu.make_async_copy(
            arrived[i],
            held.at[pl.ds(pl.multiple_of(place[3 + i] * half, half), half)],
            load_sems.at[i],
        ).start()
    blank[...] = jnp.zeros_like(blank)
    for i in range(blocks):
        pltpu.make_async_copy(
            arrived[i],
            held.at[pl.ds(pl.multiple_of(place[3 + i] * half, half), half)],
            load_sems.at[i],
        ).wait()

    def pieces(amount, first, start):
        for size in (8, 4, 2, 1):
            skipped = amount - amount % (2 * size)

            @pl.when((amount // size) % 2 == 1)
            def _():
                start(first + skipped, size)

    def issue(r, carry):
        prompt = prompts[r]
        g = prompt // PROMPTS_DEV
        slot = g * (PROMPTS_DEV + 1) + prompt - g * PROMPTS_DEV
        begin = bounds[slot]
        length = bounds[slot + 1] - begin
        begin = g * rows + begin
        full = length // PAGE
        rest = length - full * PAGE

        def copy_page(e, c):
            pltpu.make_async_copy(
                held.at[pl.ds(begin + e * PAGE, PAGE)], out.at[table[r, e]], sems.at[r]
            ).start()
            return c

        lax.fori_loop(0, full, copy_page, 0)

        @pl.when(rest > 0)
        def _():
            page = table[r, full]
            base = begin + full * PAGE

            def kept(at, size):
                pltpu.make_async_copy(
                    held.at[pl.ds(base + at, size)], out.at[page, pl.ds(at, size)], sems.at[r]
                ).start()

            def blanked(at, size):
                pltpu.make_async_copy(
                    blank.at[pl.ds(0, size)], out.at[page, pl.ds(at, size)], sems.at[r]
                ).start()

            pieces(rest, 0, kept)
            pieces(PAGE - rest, rest, blanked)

        def clear_page(e, c):
            pltpu.make_async_copy(blank, out.at[table[r, e]], sems.at[r]).start()
            return c

        lax.fori_loop((length + PAGE - 1) // PAGE, entries, clear_page, 0)
        return carry

    lax.fori_loop(0, requests, issue, 0)

    def finish(r, carry):
        pltpu.make_async_copy(
            out.at[pl.ds(0, entries)], out.at[pl.ds(0, entries)], sems.at[r]
        ).wait()
        return carry

    lax.fori_loop(0, requests, finish, 0)


def fill_pages(place, bounds, request_prompt, page_table, arrived, rows):
    requests, entries = page_table.shape
    row_shape = arrived[0].shape[1:]
    dtype = arrived[0].dtype
    blocks = len(arrived)
    held = (blocks * arrived[0].shape[0],) + row_shape
    return pl.pallas_call(
        functools.partial(page_kernel, rows, requests, entries, blocks),
        out_shape=jax.ShapeDtypeStruct((requests * entries, PAGE) + row_shape, dtype),
        in_specs=[SMEM] * 4 + [ANY] * blocks,
        out_specs=ANY,
        scratch_shapes=[
            pltpu.VMEM(held, dtype),
            pltpu.VMEM((PAGE,) + row_shape, dtype),
            pltpu.SemaphoreType.DMA((blocks,)),
            pltpu.SemaphoreType.DMA((requests,)),
        ],
        compiler_params=pltpu.CompilerParams(
            vmem_limit_bytes=math.prod(held) * 2 + (4 << 20)
        ),
        cost_estimate=pl.CostEstimate(flops=0, bytes_accessed=12 << 20, transcendentals=0),
        name="fill_pages",
    )(place, bounds, request_prompt, page_table, *arrived)


def body(
    hidden_in,
    segment_ids,
    request_prompt,
    page_table,
    ln_attn,
    w_query,
    w_key,
    w_value,
    q_gain,
    k_gain,
    w_out,
    ln_mlp,
    w_gate,
    w_up,
    w_down,
):
    parts = lax.axis_size("mp")
    groups = lax.axis_size("req")
    rows = hidden_in.shape[0] * parts
    half = rows // 2
    req = lax.axis_index("req")
    mine = lax.axis_index("mp")
    side, core = mine // 2, mine % 2
    to_core = [(i, i ^ 1) for i in range(parts)]
    to_side = [(i, i ^ 2) for i in range(parts)]
    to_pair = [(i, i ^ 1) for i in range(groups)]
    to_next = [(i, (i + 2) % groups) for i in range(groups)]

    def by_core(a):
        return lax.ppermute(a, "mp", to_core)

    def by_side(a):
        return lax.ppermute(a, "mp", to_side)

    here_x = by_side(hidden_in)
    here_c = by_core(hidden_in)
    bounds = segment_bounds(segment_ids)
    homes = []
    for step in range(groups // 2):
        for flip in (0, 1):
            for part in (0, 1):
                home = ((req ^ flip) - 2 * step) % groups
                homes.append(2 * home + (side ^ part))
    place = jnp.stack([req, side, core] + homes).astype(jnp.int32)
    cos, sin = rotation(bounds, req, side * half, rows)
    ln = ln_attn.reshape(1, -1)
    qg, kg = q_gain.reshape(1, -1), k_gain.reshape(1, -1)
    weights = (ln, w_query, w_key, w_value, qg, kg, cos, sin)
    qa, ka, va, pairs_a = project(place, hidden_in, here_c, *weights, 0)
    out_other = by_core(w_out)
    here_xc = by_core(here_x)
    qb, kb, vb, pairs_b = project(place, here_x, here_xc, *weights, 1)

    arrived = []
    moving = [pairs_a, pairs_b]
    for step in range(groups // 2):
        if step:
            moving = [lax.ppermute(a, "req", to_next) for a in moving]
        arrived += moving + [lax.ppermute(a, "req", to_pair) for a in moving]

    keep_a, send_a, keep_b, send_b = attend(place, bounds, qa, qb, ka, kb, va, vb)
    got_b = by_core(send_b)
    got_a = by_core(send_a)
    part_b = (dot(keep_b, w_out) + dot(got_b, out_other)).astype(jnp.bfloat16)
    back = by_side(part_b)
    part_a = dot(keep_a, w_out) + dot(got_a, out_other)
    after = (hidden_in.astype(jnp.float32) + part_a + back.astype(jnp.float32)).astype(
        jnp.bfloat16
    )
    down_other = by_core(w_down)

    after_x = by_side(after)
    after_c = by_core(after)
    ln2 = ln_mlp.reshape(1, -1)
    keep_a, send_a = mlp(after, after_c, ln2, w_gate, w_up)
    got_a = by_core(send_a)
    down_a = dot(keep_a, w_down) + dot(got_a, down_other)
    after_xc = by_core(after_x)
    keep_b, send_b = mlp(after_x, after_xc, ln2, w_gate, w_up)
    got_b = by_core(send_b)
    down_b = (dot(keep_b, w_down) + dot(got_b, down_other)).astype(jnp.bfloat16)
    back = by_side(down_b)
    result = (after.astype(jnp.float32) + down_a + back.astype(jnp.float32)).astype(jnp.bfloat16)
    cache = fill_pages(place, bounds, request_prompt, page_table, arrived, rows)
    return (result, cache)


def solution(mesh):
    return jax.shard_map(
        body,
        mesh=mesh,
        in_specs=(
            P(("req", "mp"), None),
            P(),
            P("req"),
            P("req", None),
            P(),
            P(None, "mp"),
            P(None, "mp"),
            P(None, "mp"),
            P(),
            P(),
            P("mp", None),
            P(),
            P(None, "mp"),
            P(None, "mp"),
            P("mp", None),
        ),
        out_specs=(P(("req", "mp"), None), P("req", None, "mp", None)),
        check_vma=False,
    )
```

```python
import functools
import math

import jax
import jax.numpy as jnp
import numpy as np
from jax import lax
from jax.experimental import pallas as pl
from jax.experimental.pallas import tpu as pltpu
from jax.sharding import PartitionSpec as P

HD = 128
PROMPTS_DEV = 3
PAGE = 16
EPS = 1e-06
THETA = 1000000.0
SMEM = pl.BlockSpec(memory_space=pltpu.SMEM)
VMEM = pl.BlockSpec(memory_space=pltpu.VMEM)
ANY = pl.BlockSpec(memory_space=pl.ANY)
FAR = pl.BlockSpec(memory_space=pltpu.HBM)
MOST = 60 << 20
BRIEF = pl.CostEstimate(flops=1, bytes_accessed=1, transcendentals=0)


def dot(a, b):
    return jnp.dot(a, b, preferred_element_type=jnp.float32)


def ordered(value, *earlier):
    return lax.optimization_barrier((value,) + earlier)[0]


def normalized(wide, gain):
    return wide * lax.rsqrt(jnp.mean(wide * wide, axis=-1, keepdims=True) + EPS) * gain


def segment_bounds(segment_ids):
    limits = jnp.arange(PROMPTS_DEV + 1, dtype=jnp.int32)
    below = segment_ids[:, None, :] < limits[None, :, None]
    return jnp.sum(below.astype(jnp.int32), axis=2).reshape(-1)


def turns(rows):
    freq = THETA ** (-(np.arange(HD // 2) * 2.0) / HD)
    angle = np.arange(rows)[:, None] * np.concatenate([freq, freq])[None, :]
    return np.cos(angle).astype(np.float32), np.sin(angle).astype(np.float32)


def angles(ids, req, first, cos_rows, sin_rows):
    row = ids[pl.ds(req, 1), :]
    begins = [jnp.sum((row < s).astype(jnp.int32)) for s in range(1, PROMPTS_DEV)]
    line = lax.broadcasted_iota(jnp.int32, (8, HD), 0)
    lane = lax.broadcasted_iota(jnp.int32, (8, HD), 1)
    turn = jnp.where(lane < HD // 2, lane, lane - HD // 2).astype(jnp.float32)
    back = jnp.zeros((8, HD), jnp.float32)
    for s, begin in enumerate(begins):
        back = jnp.where(line == s + 1, begin.astype(jnp.float32), back)
    back = back * jnp.exp(turn * (-2.0 / HD * math.log(THETA)))
    back_cos, back_sin = jnp.cos(back), jnp.sin(back)
    token = first + lax.broadcasted_iota(jnp.int32, cos_rows.shape, 0)
    less_cos, less_sin = back_cos[0:1, :], back_sin[0:1, :]
    for s, begin in enumerate(begins):
        later = token >= begin
        less_cos = jnp.where(later, back_cos[s + 1 : s + 2, :], less_cos)
        less_sin = jnp.where(later, back_sin[s + 1 : s + 2, :], less_sin)
    cosine = cos_rows * less_cos + sin_rows * less_sin
    sine = sin_rows * less_cos - cos_rows * less_sin
    first_half = lax.broadcasted_iota(jnp.int32, cos_rows.shape, 1) < HD // 2
    return cosine, jnp.where(first_half, -sine, sine), begins


def turned_heads(wide, gain_ref, cosine, sine, out, at):
    gain = gain_ref[...].astype(jnp.float32)
    for h in range(wide.shape[1] // HD):
        one = normalized(wide[:, h * HD : (h + 1) * HD], gain)
        turned = one * cosine + pltpu.roll(one, HD // 2, 1) * sine
        out[at, h * HD : (h + 1) * HD] = turned.astype(jnp.bfloat16)


def joined_heads(k, v):
    shape = (k.shape[0], k.shape[1] // HD, HD)
    return jnp.concatenate([k.reshape(shape), v.reshape(shape)], axis=-1)


def split_copies(moves, sems):
    copies, used = [], 0
    for source, target, parts in moves:
        step = source.shape[0] // parts
        group = []
        for i in range(parts):
            cut = pl.ds(i * step, step)
            group.append(pltpu.make_async_copy(source.at[cut], target.at[cut], sems.at[used]))
            used += 1
        copies.append(group)
    for group in copies:
        for copy in group:
            copy.start()
    return copies


def wait_all(group):
    for copy in group:
        copy.wait()


def keys_kernel(pieces, swapped, place, ids, *refs):
    rows_far = refs[: 1 + pieces]
    ln, wk_far, wv_far, kg, cos, sin = refs[1 + pieces : 7 + pieces]
    k, v, pairs, normed = refs[7 + pieces : 11 + pieces]
    raw, wk, wv, cos_rows, sin_rows, sems = refs[11 + pieces :]
    req, side, core = place[0], place[1], place[2]
    if swapped:
        side = 1 - side
    half = raw.shape[0]
    count = half // 2
    here = pl.ds(pl.multiple_of(side * half, half), half)
    moves = []
    at = core * count
    for i, far in enumerate(rows_far):
        step = far.shape[0]
        moves.append((far, raw.at[pl.ds(pl.multiple_of(at, step), step)], 2 if i == 0 else 1))
        at = at + step if i else (1 - core) * count
    moves += [
        (cos.at[here], cos_rows, 1),
        (sin.at[here], sin_rows, 1),
        (wk_far, wk, 4),
        (wv_far, wv, 4),
    ]
    copies = split_copies(moves, sems)
    for group in copies[:-2]:
        wait_all(group)
    gain = ln[...].astype(jnp.float32)
    normed[...] = normalized(raw[...].astype(jnp.float32), gain).astype(jnp.bfloat16)
    cosine, sine, _ = angles(ids, req, side * half, cos_rows[...], sin_rows[...])
    wait_all(copies[-2])
    turned_heads(dot(normed[...], wk[...]), kg, cosine, sine, k, slice(None))
    wait_all(copies[-1])
    v[...] = dot(normed[...], wv[...]).astype(jnp.bfloat16)
    pairs[...] = joined_heads(k[...], v[...])


def keys_of(place, ids, own, others, ln, wk, wv, kg, cos, sin, swapped):
    half, width = 2 * own.shape[0], own.shape[1]
    kv = wk.shape[1]
    bf = jnp.bfloat16
    return pl.pallas_call(
        functools.partial(keys_kernel, len(others), swapped),
        out_shape=[
            jax.ShapeDtypeStruct((half, kv), bf),
            jax.ShapeDtypeStruct((half, kv), bf),
            jax.ShapeDtypeStruct((half, kv // HD, 2 * HD), bf),
            jax.ShapeDtypeStruct((half, width), bf),
        ],
        in_specs=[SMEM, VMEM]
        + [FAR] * (1 + len(others))
        + [VMEM, FAR, FAR, VMEM, FAR, FAR],
        out_specs=[VMEM] * 4,
        scratch_shapes=[
            pltpu.VMEM((half, width), bf),
            pltpu.VMEM(wk.shape, bf),
            pltpu.VMEM(wv.shape, bf),
            pltpu.VMEM((half, HD), jnp.float32),
            pltpu.VMEM((half, HD), jnp.float32),
            pltpu.SemaphoreType.DMA((12 + 2 * len(others),)),
        ],
        compiler_params=pltpu.CompilerParams(vmem_limit_bytes=MOST),
        cost_estimate=BRIEF,
        name="keys_of",
    )(place, ids, own, *others, ln, wk, wv, kg, cos, sin)


def attend_kernel(
    place, ids, near_far, far_far, wq_far, qg, cos, sin, ka, va, kb, vb, keep, send,
    normed, wq, cos_rows, sin_rows, q, k, v, sems,
):
    req, side, core = place[0], place[1], place[2]
    half = near_far.shape[0]
    count = half // 2
    near = pl.ds(pl.multiple_of(side * half, half), half)
    far = pl.ds(pl.multiple_of((1 - side) * half, half), half)
    copies = split_copies(
        (
            (wq_far, wq, 8),
            (near_far, normed.at[near], 4),
            (far_far, normed.at[far], 4),
            (cos, cos_rows, 1),
            (sin, sin_rows, 1),
            (ka, k.at[near], 1),
            (va, v.at[near], 1),
            (kb, k.at[far], 1),
            (vb, v.at[far], 1),
        ),
        sems,
    )
    for group in copies[3:]:
        wait_all(group)
    cosine, sine, begins = angles(ids, req, 0, cos_rows[...], sin_rows[...])
    for group in copies[:3]:
        wait_all(group)
    turned_heads(dot(normed[...], wq[...]), qg, cosine, sine, q, slice(None))

    kv_here = k.shape[1] // HD
    group = q.shape[1] // k.shape[1]
    scale = 1.0 / math.sqrt(HD)
    for block in range(4):
        seen = (block + 1) * count
        token = block * count + lax.broadcasted_iota(jnp.int32, (count, seen), 0)
        column = lax.broadcasted_iota(jnp.int32, (count, seen), 1)
        start = jnp.zeros_like(token)
        for begin in begins:
            start = jnp.where(token >= begin, begin, start)
        allowed = (column <= token) & (column >= start)
        mixed = []
        for j in range(kv_here):
            lanes = slice(j * HD, (j + 1) * HD)
            for h in range(j * group, (j + 1) * group):
                scores = lax.dot_general(
                    q[block * count : seen, h * HD : (h + 1) * HD],
                    k[:seen, lanes],
                    (((1,), (1,)), ((), ())),
                    preferred_element_type=jnp.float32,
                )
                raised = jnp.where(allowed, jnp.exp(scores * scale), 0.0)
                share = 1.0 / jnp.sum(raised, axis=-1, keepdims=True)
                mixed.append(
                    dot((raised * share).astype(jnp.bfloat16), v[:seen, lanes]).astype(
                        jnp.bfloat16
                    )
                )
        for distance in range(4):
            out = send if distance % 2 else keep
            at = slice(distance // 2 * count, (distance // 2 + 1) * count)

            @pl.when((block ^ (2 * side + core)) == distance)
            def _(out=out, at=at, mixed=tuple(mixed)):
                for h, one in enumerate(mixed):
                    out[at, h * HD : (h + 1) * HD] = one


def attend(place, ids, near, far, wq, qg, cos, sin, ka, va, kb, vb):
    half, width = near.shape
    rows = 2 * half
    kv = ka.shape[1]
    bf = jnp.bfloat16
    return pl.pallas_call(
        attend_kernel,
        out_shape=[jax.ShapeDtypeStruct((half, wq.shape[1]), bf)] * 2,
        in_specs=[SMEM, VMEM, FAR, FAR, FAR, VMEM] + [FAR] * 6,
        out_specs=[VMEM] * 2,
        scratch_shapes=[
            pltpu.VMEM((rows, width), bf),
            pltpu.VMEM(wq.shape, bf),
            pltpu.VMEM((rows, HD), jnp.float32),
            pltpu.VMEM((rows, HD), jnp.float32),
            pltpu.VMEM((rows, wq.shape[1]), bf),
            pltpu.VMEM((rows, kv), bf),
            pltpu.VMEM((rows, kv), bf),
            pltpu.SemaphoreType.DMA((22,)),
        ],
        compiler_params=pltpu.CompilerParams(vmem_limit_bytes=MOST),
        cost_estimate=BRIEF,
        name="attend",
    )(place, ids, near, far, wq, qg, cos, sin, ka, va, kb, vb)


def mlp_kernel(pieces, *refs):
    ln, wg, wu, keep, send, normed = refs[pieces:]
    count = keep.shape[0]
    gain = ln[...].astype(jnp.float32)
    at = 0
    for ref in refs[:pieces]:
        normed[at : at + ref.shape[0], :] = normalized(
            ref[...].astype(jnp.float32), gain
        ).astype(jnp.bfloat16)
        at += ref.shape[0]
    rows = normed[...]
    step = 256
    for at in range(0, wg.shape[1], step):
        lanes = slice(at, at + step)
        gate = dot(rows, wg[:, lanes])
        upper = dot(rows, wu[:, lanes])
        hidden = (gate / (1.0 + jnp.exp(-gate)) * upper).astype(jnp.bfloat16)
        keep[:, lanes] = hidden[:count]
        send[:, lanes] = hidden[count:]


def mlp(first, others, ln, wg, wu):
    count, width = first.shape
    out = jax.ShapeDtypeStruct((count, wg.shape[1]), jnp.bfloat16)
    return pl.pallas_call(
        functools.partial(mlp_kernel, 1 + len(others)),
        out_shape=[out] * 2,
        in_specs=[VMEM] * (4 + len(others)),
        out_specs=[VMEM] * 2,
        scratch_shapes=[pltpu.VMEM((2 * count, width), jnp.bfloat16)],
        compiler_params=pltpu.CompilerParams(vmem_limit_bytes=24 << 20),
        cost_estimate=BRIEF,
        name="gate_up",
    )(first, *others, ln, wg, wu)


def page_kernel(rows, requests, entries, blocks, *refs):
    place, bounds, prompts, table = refs[:4]
    arrived = refs[4 : 4 + blocks]
    out, held, blank, load_sems, sems = refs[4 + blocks :]
    half = rows // 2
    loads = [
        pltpu.make_async_copy(
            ref, held.at[pl.ds(pl.multiple_of(place[3 + i] * half, half), half)], load_sems.at[i]
        )
        for i, ref in enumerate(arrived)
    ]
    for load in loads:
        load.start()
    blank[...] = jnp.zeros_like(blank)
    for load in loads:
        load.wait()

    def pieces(amount, first, start):
        for size in (8, 4, 2, 1):
            skipped = amount - amount % (2 * size)

            @pl.when((amount // size) % 2 == 1)
            def _():
                start(first + skipped, size)

    def issue(r, carry):
        prompt = prompts[r]
        g = prompt // PROMPTS_DEV
        slot = g * (PROMPTS_DEV + 1) + prompt - g * PROMPTS_DEV
        begin = bounds[slot]
        length = bounds[slot + 1] - begin
        begin = g * rows + begin
        full = length // PAGE
        rest = length - full * PAGE

        def copy_page(e, c):
            pltpu.make_async_copy(
                held.at[pl.ds(begin + e * PAGE, PAGE)], out.at[table[r, e]], sems.at[r]
            ).start()
            return c

        lax.fori_loop(0, full, copy_page, 0)

        @pl.when(rest > 0)
        def _():
            page = table[r, full]
            base = begin + full * PAGE

            def kept(at, size):
                pltpu.make_async_copy(
                    held.at[pl.ds(base + at, size)], out.at[page, pl.ds(at, size)], sems.at[r]
                ).start()

            def blanked(at, size):
                pltpu.make_async_copy(
                    blank.at[pl.ds(0, size)], out.at[page, pl.ds(at, size)], sems.at[r]
                ).start()

            pieces(rest, 0, kept)
            pieces(PAGE - rest, rest, blanked)

        def clear_page(e, c):
            pltpu.make_async_copy(blank, out.at[table[r, e]], sems.at[r]).start()
            return c

        lax.fori_loop((length + PAGE - 1) // PAGE, entries, clear_page, 0)
        return carry

    lax.fori_loop(0, requests, issue, 0)

    def finish(r, carry):
        pltpu.make_async_copy(
            out.at[pl.ds(0, entries)], out.at[pl.ds(0, entries)], sems.at[r]
        ).wait()
        return carry

    lax.fori_loop(0, requests, finish, 0)


def fill_pages(place, bounds, request_prompt, page_table, arrived, rows):
    requests, entries = page_table.shape
    row_shape, dtype = arrived[0].shape[1:], arrived[0].dtype
    blocks = len(arrived)
    return pl.pallas_call(
        functools.partial(page_kernel, rows, requests, entries, blocks),
        out_shape=jax.ShapeDtypeStruct((requests * entries, PAGE) + row_shape, dtype),
        in_specs=[SMEM] * 4 + [FAR] * blocks,
        out_specs=ANY,
        scratch_shapes=[
            pltpu.VMEM((blocks * rows // 2,) + row_shape, dtype),
            pltpu.VMEM((PAGE,) + row_shape, dtype),
            pltpu.SemaphoreType.DMA((blocks,)),
            pltpu.SemaphoreType.DMA((requests,)),
        ],
        compiler_params=pltpu.CompilerParams(vmem_limit_bytes=MOST),
        cost_estimate=BRIEF,
        name="fill_pages",
    )(place, bounds, request_prompt, page_table, *arrived)


def body(
    hidden_in,
    segment_ids,
    request_prompt,
    page_table,
    ln_attn,
    w_query,
    w_key,
    w_value,
    q_gain,
    k_gain,
    w_out,
    ln_mlp,
    w_gate,
    w_up,
    w_down,
):
    parts = lax.axis_size("mp")
    groups = lax.axis_size("req")
    rows = hidden_in.shape[0] * parts
    half = rows // 2
    req = lax.axis_index("req")
    mine = lax.axis_index("mp")
    side, core = mine // 2, mine % 2
    to_core = [(i, i ^ 1) for i in range(parts)]
    to_side = [(i, i ^ 2) for i in range(parts)]
    to_pair = [(i, i ^ 1) for i in range(groups)]
    to_next = [(i, (i + 2) % groups) for i in range(groups)]

    def by_core(a):
        return lax.ppermute(a, "mp", to_core)

    def by_core_in_pieces(a):
        return [by_core(piece) for piece in jnp.split(a, 4)]

    def by_side(a):
        return lax.ppermute(a, "mp", to_side)

    def forward(a):
        return lax.ppermute(a, "req", to_next)

    def flipped(a):
        return lax.ppermute(a, "req", to_pair)

    here_x = by_side(hidden_in)
    here_c = by_core_in_pieces(hidden_in)
    steps = groups // 2
    homes = []
    for flip in (0, 1):
        for part in (0, 1):
            for step in range(steps):
                home = ((req ^ flip) - 2 * step) % groups
                homes.append(2 * home + (side ^ part))
    place = jnp.stack([req, side, core] + homes).astype(jnp.int32)
    ln = ln_attn.reshape(1, -1)
    qg, kg = q_gain.reshape(1, -1), k_gain.reshape(1, -1)
    cos, sin = turns(rows)
    tables = (ln, w_key, w_value, kg, cos, sin)
    ka, va, pairs_a, near = keys_of(place, segment_ids, hidden_in, here_c, *tables, False)
    line_a, flips_a = [pairs_a, forward(pairs_a)], [flipped(pairs_a)]
    bounds = segment_bounds(ordered(segment_ids, pairs_a))
    here_x = ordered(here_x, bounds, line_a[1], flips_a[0])
    here_xc = by_core(here_x)
    out_other = by_core(ordered(w_out, here_xc))
    kb, vb, pairs_b, far = keys_of(place, segment_ids, here_x, [here_xc], *tables, True)
    line_b, flips_b = [pairs_b, forward(pairs_b)], [flipped(pairs_b)]
    line_a.append(forward(line_a[1]))
    flips_a.append(flipped(line_a[1]))
    keep, send = attend(
        place, segment_ids, near, far, w_query, qg, cos, sin, ka, va, kb, vb
    )
    send = ordered(send, line_a[2], flips_a[1], line_b[1], flips_b[0])
    got = by_core(send)
    part_b = (dot(keep[half // 2 :], w_out) + dot(got[half // 2 :], out_other)).astype(
        jnp.bfloat16
    )
    back = by_side(part_b)
    keep, got = ordered(keep, part_b), ordered(got, part_b)
    part_a = dot(keep[: half // 2], w_out) + dot(got[: half // 2], out_other)
    line_a.append(forward(line_a[2]))
    line_b.append(forward(line_b[1]))
    flips_a.append(flipped(line_a[2]))
    flips_b.append(flipped(line_b[1]))
    back = ordered(back, part_a, line_a[3], flips_a[2], line_b[2], flips_b[1])
    after = (hidden_in.astype(jnp.float32) + part_a + back.astype(jnp.float32)).astype(
        jnp.bfloat16
    )

    after_x = by_side(after)
    after_c = by_core_in_pieces(after)
    ln2 = ln_mlp.reshape(1, -1)
    line_b.append(forward(line_b[2]))
    flips_a.append(flipped(line_a[3]))
    flips_b.append(flipped(line_b[2]))
    keep_a, send_a = mlp(after, after_c, ln2, w_gate, w_up)
    down_other = by_core(ordered(w_down, send_a))
    after_x = ordered(after_x, keep_a, line_b[3], flips_a[3], flips_b[2])
    after_xc = by_core(after_x)
    flips_b.append(flipped(line_b[3]))
    for step in range(4, steps):
        line_a.append(forward(line_a[step - 1]))
        line_b.append(forward(line_b[step - 1]))
        flips_a.append(flipped(line_a[step]))
        flips_b.append(flipped(line_b[step]))
    keep_b, send_b = mlp(after_x, [after_xc], ln2, w_gate, w_up)
    got_b = by_core(send_b)
    got_a = by_core(send_a)
    down_b = (dot(keep_b, w_down) + dot(got_b, down_other)).astype(jnp.bfloat16)
    back = by_side(down_b)
    got_a = ordered(got_a, down_b)
    down_a = dot(keep_a, w_down) + dot(got_a, down_other)
    arrived = line_a + line_b + flips_a + flips_b
    bounds = ordered(bounds, down_b)
    cache = fill_pages(place, bounds, request_prompt, page_table, arrived, rows)
    result = (after.astype(jnp.float32) + down_a + back.astype(jnp.float32)).astype(jnp.bfloat16)
    return (result, cache)


def solution(mesh):
    return jax.shard_map(
        body,
        mesh=mesh,
        in_specs=(
            P(("req", "mp"), None),
            P(),
            P("req"),
            P("req", None),
            P(),
            P(None, "mp"),
            P(None, "mp"),
            P(None, "mp"),
            P(),
            P(),
            P("mp", None),
            P(),
            P(None, "mp"),
            P(None, "mp"),
            P("mp", None),
        ),
        out_specs=(P(("req", "mp"), None), P("req", None, "mp", None)),
        check_vma=False,
    )
```

```python
import functools
import math

import jax
import jax.numpy as jnp
import numpy as np
from jax import lax
from jax.experimental import pallas as pl
from jax.experimental.pallas import tpu as pltpu
from jax.sharding import PartitionSpec as P

HD = 128
PROMPTS_DEV = 3
PAGE = 16
EPS = 1e-06
THETA = 1000000.0
SMEM = pl.BlockSpec(memory_space=pltpu.SMEM)
VMEM = pl.BlockSpec(memory_space=pltpu.VMEM)
ANY = pl.BlockSpec(memory_space=pl.ANY)
FAR = pl.BlockSpec(memory_space=pltpu.HBM)
MOST = 63 * 10**6
BRIEF = pl.CostEstimate(flops=1, bytes_accessed=1, transcendentals=0)


def dot(a, b):
    return jnp.dot(a, b, preferred_element_type=jnp.float32)


def ordered(value, *earlier):
    return lax.optimization_barrier((value,) + earlier)[0]


def normalized(wide, gain):
    return wide * lax.rsqrt(jnp.mean(wide * wide, axis=-1, keepdims=True) + EPS) * gain


def segment_bounds(segment_ids):
    limits = jnp.arange(PROMPTS_DEV + 1, dtype=jnp.int32)
    below = segment_ids[:, None, :] < limits[None, :, None]
    return jnp.sum(below.astype(jnp.int32), axis=2).reshape(-1)


def turns(rows):
    freq = THETA ** (-(np.arange(HD // 2) * 2.0) / HD)
    angle = np.arange(rows)[:, None] * np.concatenate([freq, freq])[None, :]
    return np.cos(angle).astype(np.float32), np.sin(angle).astype(np.float32)


def angles(ids, req, first, cos_rows, sin_rows):
    row = ids[pl.ds(req, 1), :]
    begins = [jnp.sum((row < s).astype(jnp.int32)) for s in range(1, PROMPTS_DEV)]
    line = lax.broadcasted_iota(jnp.int32, (8, HD), 0)
    lane = lax.broadcasted_iota(jnp.int32, (8, HD), 1)
    turn = jnp.where(lane < HD // 2, lane, lane - HD // 2).astype(jnp.float32)
    back = jnp.zeros((8, HD), jnp.float32)
    for s, begin in enumerate(begins):
        back = jnp.where(line == s + 1, begin.astype(jnp.float32), back)
    back = back * jnp.exp(turn * (-2.0 / HD * math.log(THETA)))
    back_cos, back_sin = jnp.cos(back), jnp.sin(back)
    token = first + lax.broadcasted_iota(jnp.int32, cos_rows.shape, 0)
    less_cos, less_sin = back_cos[0:1, :], back_sin[0:1, :]
    for s, begin in enumerate(begins):
        later = token >= begin
        less_cos = jnp.where(later, back_cos[s + 1 : s + 2, :], less_cos)
        less_sin = jnp.where(later, back_sin[s + 1 : s + 2, :], less_sin)
    cosine = cos_rows * less_cos + sin_rows * less_sin
    sine = sin_rows * less_cos - cos_rows * less_sin
    first_half = lax.broadcasted_iota(jnp.int32, cos_rows.shape, 1) < HD // 2
    return cosine, jnp.where(first_half, -sine, sine), begins


def turned_heads(wide, gain_ref, cosine, sine, out, at):
    gain = gain_ref[...].astype(jnp.float32)
    for h in range(wide.shape[1] // HD):
        one = normalized(wide[:, h * HD : (h + 1) * HD], gain)
        turned = one * cosine + pltpu.roll(one, HD // 2, 1) * sine
        out[at, h * HD : (h + 1) * HD] = turned.astype(jnp.bfloat16)


def joined_heads(k, v):
    shape = (k.shape[0], k.shape[1] // HD, HD)
    return jnp.concatenate([k.reshape(shape), v.reshape(shape)], axis=-1)


def split_copies(moves, sems):
    copies, used = [], 0
    for source, target, parts in moves:
        step = source.shape[0] // parts
        group = []
        for i in range(parts):
            cut = pl.ds(i * step, step)
            group.append(pltpu.make_async_copy(source.at[cut], target.at[cut], sems.at[used]))
            used += 1
        copies.append(group)
    for group in copies:
        for copy in group:
            copy.start()
    return copies


def wait_all(group):
    for copy in group:
        copy.wait()


def project_rows(raw, ln, wk, wv, wq, qg, kg, cosine, sine, waits, q, k, v, pairs, at):
    gain = ln[...].astype(jnp.float32)
    rows = normalized(raw[...].astype(jnp.float32), gain).astype(jnp.bfloat16)
    wait_all(waits[0])
    turned_heads(dot(rows, wk[...]), kg, cosine, sine, k, at)
    wait_all(waits[1])
    v[at, :] = dot(rows, wv[...]).astype(jnp.bfloat16)
    pairs[...] = joined_heads(k[at, :], v[at, :])
    wait_all(waits[2])
    turned_heads(dot(rows, wq[...]), qg, cosine, sine, q, at)


def first_kernel(pieces, place, ids, *refs):
    rows_far = refs[: 1 + pieces]
    ln, wq_far, wk_far, wv_far, qg, kg, cos, sin = refs[1 + pieces : 9 + pieces]
    q, k, v, pairs, raw, wq, wk, wv, cos_rows, sin_rows, sems = refs[9 + pieces :]
    req, side, core = place[0], place[1], place[2]
    half = raw.shape[0]
    count = half // 2
    here = pl.ds(pl.multiple_of(side * half, half), half)
    moves = []
    at = core * count
    for i, far in enumerate(rows_far):
        step = far.shape[0]
        moves.append((far, raw.at[pl.ds(pl.multiple_of(at, step), step)], 1))
        at = at + step if i else (1 - core) * count
    moves += [
        (cos.at[here], cos_rows, 1),
        (sin.at[here], sin_rows, 1),
        (wk_far, wk, 1),
        (wv_far, wv, 1),
        (wq_far, wq, 1),
    ]
    copies = split_copies(moves, sems)
    for group in copies[:-3]:
        wait_all(group)
    cosine, sine, _ = angles(ids, req, side * half, cos_rows[...], sin_rows[...])
    project_rows(
        raw, ln, wk, wv, wq, qg, kg, cosine, sine, copies[-3:], q, k, v, pairs, slice(None)
    )


def first_half(place, ids, own, others, ln, wq, wk, wv, qg, kg, cos, sin):
    half, width = 2 * own.shape[0], own.shape[1]
    kv = wk.shape[1]
    bf = jnp.bfloat16
    return pl.pallas_call(
        functools.partial(first_kernel, len(others)),
        out_shape=[
            jax.ShapeDtypeStruct((half, wq.shape[1]), bf),
            jax.ShapeDtypeStruct((half, kv), bf),
            jax.ShapeDtypeStruct((half, kv), bf),
            jax.ShapeDtypeStruct((half, kv // HD, 2 * HD), bf),
        ],
        in_specs=[SMEM, VMEM]
        + [FAR] * (1 + len(others))
        + [VMEM, FAR, FAR, FAR, VMEM, VMEM, FAR, FAR],
        out_specs=[VMEM] * 4,
        scratch_shapes=[
            pltpu.VMEM((half, width), bf),
            pltpu.VMEM(wq.shape, bf),
            pltpu.VMEM(wk.shape, bf),
            pltpu.VMEM(wv.shape, bf),
            pltpu.VMEM((half, HD), jnp.float32),
            pltpu.VMEM((half, HD), jnp.float32),
            pltpu.SemaphoreType.DMA((6 + len(others),)),
        ],
        compiler_params=pltpu.CompilerParams(vmem_limit_bytes=MOST),
        cost_estimate=BRIEF,
        name="first_half",
    )(place, ids, own, *others, ln, wq, wk, wv, qg, kg, cos, sin)


def second_kernel(
    place, ids, mine_far, other_far, ln, wq_far, wk_far, wv_far, qg, kg, cos, sin,
    qa, ka, va, pairs, keep, send,
    raw, wq, wk, wv, cos_rows, sin_rows, q, k, v, mixed, sems,
):
    req, side, core = place[0], place[1], place[2]
    half = raw.shape[0]
    count = half // 2
    near = pl.ds(pl.multiple_of(side * half, half), half)
    far = pl.ds(pl.multiple_of((1 - side) * half, half), half)
    copies = split_copies(
        (
            (mine_far, raw.at[pl.ds(pl.multiple_of(core * count, count), count)], 1),
            (other_far, raw.at[pl.ds(pl.multiple_of((1 - core) * count, count), count)], 1),
            (cos.at[far], cos_rows, 1),
            (sin.at[far], sin_rows, 1),
            (wk_far, wk, 1),
            (wv_far, wv, 1),
            (wq_far, wq, 1),
            (ka, k.at[near], 1),
            (qa, q.at[near], 1),
            (va, v.at[near], 1),
        ),
        sems,
    )
    for group in copies[:4]:
        wait_all(group)
    cosine, sine, begins = angles(ids, req, (1 - side) * half, cos_rows[...], sin_rows[...])
    project_rows(
        raw, ln, wk, wv, wq, qg, kg, cosine, sine, copies[4:7], q, k, v, pairs, far
    )
    for group in copies[7:]:
        wait_all(group)
    kv_here = k.shape[1] // HD
    group = q.shape[1] // k.shape[1]
    scale = 1.0 / math.sqrt(HD)
    for block in range(2):
        seen = (block + 1) * half
        here = slice(block * half, seen)
        token = block * half + lax.broadcasted_iota(jnp.int32, (half, seen), 0)
        column = lax.broadcasted_iota(jnp.int32, (half, seen), 1)
        start = jnp.zeros_like(token)
        for begin in begins:
            start = jnp.where(token >= begin, begin, start)
        allowed = (column <= token) & (column >= start)
        for j in range(kv_here):
            lanes = slice(j * HD, (j + 1) * HD)
            heads = range(j * group, (j + 1) * group)
            scores = lax.dot_general(
                jnp.concatenate([q[here, h * HD : (h + 1) * HD] for h in heads], axis=0),
                k[:seen, lanes],
                (((1,), (1,)), ((), ())),
                preferred_element_type=jnp.float32,
            )
            raised = [
                jnp.where(allowed, jnp.exp(scores[i * half : (i + 1) * half] * scale), 0.0)
                for i in range(group)
            ]
            summed = dot(
                jnp.concatenate([r.astype(jnp.bfloat16) for r in raised], axis=0),
                v[:seen, lanes],
            )
            for i, h in enumerate(heads):
                share = 1.0 / jnp.sum(raised[i], axis=-1, keepdims=True)
                mixed[here, h * HD : (h + 1) * HD] = (
                    summed[i * half : (i + 1) * half] * share
                ).astype(jnp.bfloat16)
    mine = 2 * side + core
    for distance in range(4):
        out = send if distance % 2 else keep
        at = pl.ds(pl.multiple_of((mine ^ distance) * count, count), count)
        out[distance // 2 * count : (distance // 2 + 1) * count, :] = mixed[at, :]


def second_half(place, ids, mine, other, ln, wq, wk, wv, qg, kg, cos, sin, qa, ka, va):
    half, width = 2 * mine.shape[0], mine.shape[1]
    kv = wk.shape[1]
    bf = jnp.bfloat16
    return pl.pallas_call(
        second_kernel,
        out_shape=[jax.ShapeDtypeStruct((half, kv // HD, 2 * HD), bf)]
        + [jax.ShapeDtypeStruct((half, wq.shape[1]), bf)] * 2,
        in_specs=[SMEM, VMEM, FAR, FAR, VMEM, FAR, FAR, FAR, VMEM, VMEM] + [FAR] * 5,
        out_specs=[VMEM] * 3,
        scratch_shapes=[
            pltpu.VMEM((half, width), bf),
            pltpu.VMEM(wq.shape, bf),
            pltpu.VMEM(wk.shape, bf),
            pltpu.VMEM(wv.shape, bf),
            pltpu.VMEM((half, HD), jnp.float32),
            pltpu.VMEM((half, HD), jnp.float32),
            pltpu.VMEM((2 * half, wq.shape[1]), bf),
            pltpu.VMEM((2 * half, kv), bf),
            pltpu.VMEM((2 * half, kv), bf),
            pltpu.VMEM((2 * half, wq.shape[1]), bf),
            pltpu.SemaphoreType.DMA((10,)),
        ],
        compiler_params=pltpu.CompilerParams(vmem_limit_bytes=MOST),
        cost_estimate=BRIEF,
        name="second_half",
    )(place, ids, mine, other, ln, wq, wk, wv, qg, kg, cos, sin, qa, ka, va)


def mlp_kernel(pieces, *refs):
    ln, wg, wu, keep, send, normed = refs[pieces:]
    count = keep.shape[0]
    gain = ln[...].astype(jnp.float32)
    at = 0
    for ref in refs[:pieces]:
        normed[at : at + ref.shape[0], :] = normalized(
            ref[...].astype(jnp.float32), gain
        ).astype(jnp.bfloat16)
        at += ref.shape[0]
    rows = normed[...]
    step = 256
    for at in range(0, wg.shape[1], step):
        lanes = slice(at, at + step)
        gate = dot(rows, wg[:, lanes])
        upper = dot(rows, wu[:, lanes])
        hidden = (gate / (1.0 + jnp.exp(-gate)) * upper).astype(jnp.bfloat16)
        keep[:, lanes] = hidden[:count]
        send[:, lanes] = hidden[count:]


def mlp(first, others, ln, wg, wu):
    count, width = first.shape
    out = jax.ShapeDtypeStruct((count, wg.shape[1]), jnp.bfloat16)
    return pl.pallas_call(
        functools.partial(mlp_kernel, 1 + len(others)),
        out_shape=[out] * 2,
        in_specs=[VMEM] * (4 + len(others)),
        out_specs=[VMEM] * 2,
        scratch_shapes=[pltpu.VMEM((2 * count, width), jnp.bfloat16)],
        compiler_params=pltpu.CompilerParams(vmem_limit_bytes=24 << 20),
        cost_estimate=BRIEF,
        name="gate_up",
    )(first, *others, ln, wg, wu)


def page_kernel(rows, requests, entries, blocks, *refs):
    homes, bounds, prompts, table = refs[:4]
    arrived = refs[4 : 4 + blocks]
    out, held, blank, where, load_sems, sems = refs[-6:]
    half = rows // 2
    side = homes[blocks // 2]
    loads = [
        pltpu.make_async_copy(
            ref,
            held.at[pl.ds(pl.multiple_of(i // 2 * rows + (side ^ (i % 2)) * half, half), half)],
            load_sems.at[i],
        )
        for i, ref in enumerate(arrived)
    ]
    for load in loads:
        load.start()
    blank[...] = jnp.zeros_like(blank)

    def forget(g, carry):
        where[g] = -1
        return carry

    lax.fori_loop(0, where.shape[0], forget, 0)
    for i in range(blocks // 2):
        where[homes[i]] = i

    def taken(r):
        return where[prompts[r] // PROMPTS_DEV] >= 0

    def span(r):
        prompt = prompts[r]
        g = prompt // PROMPTS_DEV
        slot = g * (PROMPTS_DEV + 1) + prompt - g * PROMPTS_DEV
        begin = bounds[slot]
        return where[g] * rows + begin, bounds[slot + 1] - begin

    def clear(r, carry):
        def clear_page(e, c):
            pltpu.make_async_copy(blank, out.at[table[r * entries + e]], sems.at[r]).start()
            return c

        @pl.when(taken(r))
        def _():
            lax.fori_loop((span(r)[1] + PAGE - 1) // PAGE, entries, clear_page, 0)

        return carry

    lax.fori_loop(0, requests, clear, 0)
    for load in loads:
        load.wait()

    def pieces(amount, first, start):
        for size in (8, 4, 2, 1):
            skipped = amount - amount % (2 * size)

            @pl.when((amount // size) % 2 == 1)
            def _():
                start(first + skipped, size)

    def issue(r, carry):
        @pl.when(taken(r))
        def _():
            issue_one(r)

        return carry

    def issue_one(r):
        begin, length = span(r)
        full = length // PAGE
        rest = length - full * PAGE

        def copy_page(e, c):
            pltpu.make_async_copy(
                held.at[pl.ds(begin + e * PAGE, PAGE)], out.at[table[r * entries + e]], sems.at[r]
            ).start()
            return c

        lax.fori_loop(0, full, copy_page, 0)

        @pl.when(rest > 0)
        def _():
            page = table[r * entries + full]
            base = begin + full * PAGE

            def kept(at, size):
                pltpu.make_async_copy(
                    held.at[pl.ds(base + at, size)], out.at[page, pl.ds(at, size)], sems.at[r]
                ).start()

            def blanked(at, size):
                pltpu.make_async_copy(
                    blank.at[pl.ds(0, size)], out.at[page, pl.ds(at, size)], sems.at[r]
                ).start()

            pieces(rest, 0, kept)
            pieces(PAGE - rest, rest, blanked)

    lax.fori_loop(0, requests, issue, 0)

    def finish(r, carry):
        @pl.when(taken(r))
        def _():
            pltpu.make_async_copy(
                out.at[pl.ds(0, entries)], out.at[pl.ds(0, entries)], sems.at[r]
            ).wait()

        return carry

    lax.fori_loop(0, requests, finish, 0)


def fill_pages(bounds, request_prompt, page_table, arrived, homes, rows, cache=None):
    requests = request_prompt.shape[0]
    entries = page_table.shape[0] // requests
    row_shape, dtype = arrived[0].shape[1:], arrived[0].dtype
    blocks = len(arrived)
    given = [] if cache is None else [cache]
    held = (blocks // 2 * rows,) + row_shape
    return pl.pallas_call(
        functools.partial(page_kernel, rows, requests, entries, blocks),
        out_shape=jax.ShapeDtypeStruct((requests * entries, PAGE) + row_shape, dtype),
        in_specs=[SMEM] * 4 + [FAR] * blocks + [ANY] * len(given),
        out_specs=ANY,
        scratch_shapes=[
            pltpu.VMEM(held, dtype),
            pltpu.VMEM((PAGE,) + row_shape, dtype),
            pltpu.SMEM((bounds.shape[0] // (PROMPTS_DEV + 1),), jnp.int32),
            pltpu.SemaphoreType.DMA((blocks,)),
            pltpu.SemaphoreType.DMA((requests,)),
        ],
        input_output_aliases={4 + blocks: 0} if given else {},
        compiler_params=pltpu.CompilerParams(vmem_limit_bytes=MOST),
        cost_estimate=BRIEF,
        name="fill_pages",
    )(homes, bounds, request_prompt, page_table, *arrived, *given)


def body(
    hidden_in,
    segment_ids,
    request_prompt,
    page_table,
    ln_attn,
    w_query,
    w_key,
    w_value,
    q_gain,
    k_gain,
    w_out,
    ln_mlp,
    w_gate,
    w_up,
    w_down,
):
    parts = lax.axis_size("mp")
    groups = lax.axis_size("req")
    rows = hidden_in.shape[0] * parts
    half = rows // 2
    req = lax.axis_index("req")
    mine = lax.axis_index("mp")
    side, core = mine // 2, mine % 2
    to_core = [(i, i ^ 1) for i in range(parts)]
    to_side = [(i, i ^ 2) for i in range(parts)]
    to_pair = [(i, i ^ 1) for i in range(groups)]
    to_next = [(i, (i + 2) % groups) for i in range(groups)]

    def by_core(a):
        return lax.ppermute(a, "mp", to_core)

    def by_core_in_pieces(a):
        return [by_core(piece) for piece in jnp.split(a, 2)]

    def by_side(a):
        return lax.ppermute(a, "mp", to_side)

    def forward(a):
        return lax.ppermute(a, "req", to_next)

    def flipped(a):
        return lax.ppermute(a, "req", to_pair)

    here_x = by_side(hidden_in)
    here_c = by_core_in_pieces(hidden_in)
    steps = groups // 2
    homes = [(req - 2 * step) % groups for step in range(steps)]
    homes += [((req ^ 1) - 2 * step) % groups for step in range(steps)]
    place = jnp.stack([req, side, core]).astype(jnp.int32)
    ln = ln_attn.reshape(1, -1)
    qg, kg = q_gain.reshape(1, -1), k_gain.reshape(1, -1)
    cos, sin = turns(rows)
    tables = (ln, w_query, w_key, w_value, qg, kg, cos, sin)
    qa, ka, va, pairs_a = first_half(place, segment_ids, hidden_in, here_c, *tables)
    line_a, flips_a = [pairs_a, forward(pairs_a)], [flipped(pairs_a)]
    bounds = segment_bounds(ordered(segment_ids, ka))
    out_other = by_core(w_out)
    first_homes = jnp.stack(homes[: steps - 1] + homes[steps : 2 * steps - 2] + [side])
    last_homes = jnp.stack([homes[steps - 1], homes[-2], homes[-1], side])
    page_table = page_table.reshape(-1)
    here_x, bounds, first_homes, last_homes, page_table = lax.optimization_barrier(
        (here_x, bounds, first_homes.astype(jnp.int32), last_homes.astype(jnp.int32), page_table)
    )
    here_x = ordered(here_x, out_other)
    here_xc = by_core(here_x)
    down_other = by_core(ordered(w_down, here_xc))
    pairs_b, keep, send = second_half(
        place, segment_ids, here_x, here_xc, *tables, qa, ka, va
    )
    send = ordered(send, line_a[1], flips_a[0])
    got = by_core(send)
    part_b = (dot(keep[half // 2 :], w_out) + dot(got[half // 2 :], out_other)).astype(
        jnp.bfloat16
    )
    part_b = ordered(part_b, down_other)
    back = by_side(part_b)
    keep, got = ordered(keep, part_b), ordered(got, part_b)
    part_a = dot(keep[: half // 2], w_out) + dot(got[: half // 2], out_other)
    back = ordered(back, part_a)
    after = (hidden_in.astype(jnp.float32) + part_a + back.astype(jnp.float32)).astype(
        jnp.bfloat16
    )


    def advance(line, flips):
        flips.append(flipped(line[-1]))
        line.append(forward(line[-1]))

    line_b, flips_b = [pairs_b], []
    line_a[1], line_b[0] = ordered(line_a[1], part_b), ordered(line_b[0], part_b)
    advance(line_a, flips_a)
    advance(line_b, flips_b)
    after = ordered(after, line_a[-1], line_b[-1], flips_a[-1], flips_b[-1])
    after_x = by_side(after)
    after_c = [by_core(after)]
    ln2 = ln_mlp.reshape(1, -1)
    line_a[-1], line_b[-1] = ordered((line_a[-1], line_b[-1]), after)
    advance(line_a, flips_a)
    advance(line_b, flips_b)
    keep_a, send_a = mlp(after, after_c, ln2, w_gate, w_up)
    after_x = ordered(after_x, keep_a)
    after_x = ordered(after_x, line_a[-1], line_b[-1], flips_a[-1], flips_b[-1])
    after_xc = by_core(after_x)
    got_a = by_core(send_a)
    down_a = dot(keep_a, w_down) + dot(got_a, down_other)
    after_xc = ordered(after_xc, down_a)
    keep_b, send_b = mlp(after_x, [after_xc], ln2, w_gate, w_up)
    line_a[-1], line_b[-1], flips_a[-1] = ordered(
        (line_a[-1], line_b[-1], flips_a[-1]), after_x
    )
    for step in range(4, steps):
        advance(line_a, flips_a)
        advance(line_b, flips_b)
    flips_a.append(forward(flips_a[-1]))
    advance(line_b, flips_b)
    got_b = by_core(send_b)
    down_b = (dot(keep_b, w_down) + dot(got_b, down_other)).astype(jnp.bfloat16)
    back = by_side(down_b)
    tables = (ordered(bounds, down_b, line_b[-1]), request_prompt, page_table)
    blocks = list(zip(line_a, line_b))[: steps - 1] + list(zip(flips_a, flips_b))[: steps - 2]
    cache = fill_pages(
        *tables,
        [part for block in blocks for part in block],
        first_homes,
        rows,
    )
    flips_b.append(flipped(line_b[-1]))
    cache = fill_pages(
        *tables,
        [line_a[-1], line_b[-1], flips_a[-2], flips_b[-2], flips_a[-1], flips_b[-1]],
        last_homes,
        rows,
        cache,
    )
    result = (after.astype(jnp.float32) + down_a + back.astype(jnp.float32)).astype(jnp.bfloat16)
    return (result, cache)


def solution(mesh):
    return jax.shard_map(
        body,
        mesh=mesh,
        in_specs=(
            P(("req", "mp"), None),
            P(),
            P("req"),
            P("req", None),
            P(),
            P(None, "mp"),
            P(None, "mp"),
            P(None, "mp"),
            P(),
            P(),
            P("mp", None),
            P(),
            P(None, "mp"),
            P(None, "mp"),
            P("mp", None),
        ),
        out_specs=(P(("req", "mp"), None), P("req", None, "mp", None)),
        check_vma=False,
    )
```

```python
import functools
import math

import jax
import jax.numpy as jnp
import numpy as np
from jax import lax
from jax.experimental import pallas as pl
from jax.experimental.pallas import tpu as pltpu
from jax.sharding import PartitionSpec as P

HD = 128
PROMPTS_DEV = 3
PAGE = 16
EPS = 1e-06
THETA = 1000000.0
SMEM = pl.BlockSpec(memory_space=pltpu.SMEM)
VMEM = pl.BlockSpec(memory_space=pltpu.VMEM)
ANY = pl.BlockSpec(memory_space=pl.ANY)
FAR = pl.BlockSpec(memory_space=pltpu.HBM)
MOST = 63 * 10**6
BRIEF = pl.CostEstimate(flops=1, bytes_accessed=1, transcendentals=0)


def dot(a, b):
    return jnp.dot(a, b, preferred_element_type=jnp.float32)


def ordered(value, *earlier):
    return lax.optimization_barrier((value,) + earlier)[0]


def normalized(wide, gain):
    return wide * lax.rsqrt(jnp.mean(wide * wide, axis=-1, keepdims=True) + EPS) * gain


def segment_bounds(segment_ids):
    limits = jnp.arange(PROMPTS_DEV + 1, dtype=jnp.int32)
    below = segment_ids[:, None, :] < limits[None, :, None]
    return jnp.sum(below.astype(jnp.int32), axis=2).reshape(-1)


def turns(rows):
    freq = THETA ** (-(np.arange(HD // 2) * 2.0) / HD)
    angle = np.arange(rows)[:, None] * np.concatenate([freq, freq])[None, :]
    return np.cos(angle).astype(np.float32), np.sin(angle).astype(np.float32)


def angles(ids, req, first, cos_rows, sin_rows):
    row = ids[pl.ds(req, 1), :]
    begins = [jnp.sum((row < s).astype(jnp.int32)) for s in range(1, PROMPTS_DEV)]
    line = lax.broadcasted_iota(jnp.int32, (8, HD), 0)
    lane = lax.broadcasted_iota(jnp.int32, (8, HD), 1)
    turn = jnp.where(lane < HD // 2, lane, lane - HD // 2).astype(jnp.float32)
    back = jnp.zeros((8, HD), jnp.float32)
    for s, begin in enumerate(begins):
        back = jnp.where(line == s + 1, begin.astype(jnp.float32), back)
    back = back * jnp.exp(turn * (-2.0 / HD * math.log(THETA)))
    back_cos, back_sin = jnp.cos(back), jnp.sin(back)
    token = first + lax.broadcasted_iota(jnp.int32, cos_rows.shape, 0)
    less_cos, less_sin = back_cos[0:1, :], back_sin[0:1, :]
    for s, begin in enumerate(begins):
        later = token >= begin
        less_cos = jnp.where(later, back_cos[s + 1 : s + 2, :], less_cos)
        less_sin = jnp.where(later, back_sin[s + 1 : s + 2, :], less_sin)
    cosine = cos_rows * less_cos + sin_rows * less_sin
    sine = sin_rows * less_cos - cos_rows * less_sin
    first_half = lax.broadcasted_iota(jnp.int32, cos_rows.shape, 1) < HD // 2
    return cosine, jnp.where(first_half, -sine, sine), begins


def turned_heads(wide, gain_ref, cosine, sine, out, at):
    gain = gain_ref[...].astype(jnp.float32)
    for h in range(wide.shape[1] // HD):
        one = normalized(wide[:, h * HD : (h + 1) * HD], gain)
        turned = one * cosine + pltpu.roll(one, HD // 2, 1) * sine
        out[at, h * HD : (h + 1) * HD] = turned.astype(jnp.bfloat16)


def joined_heads(k, v):
    shape = (k.shape[0], k.shape[1] // HD, HD)
    return jnp.concatenate([k.reshape(shape), v.reshape(shape)], axis=-1)


def split_copies(moves, sems):
    copies, used = [], 0
    for source, target, parts in moves:
        step = source.shape[0] // parts
        group = []
        for i in range(parts):
            cut = pl.ds(i * step, step)
            group.append(pltpu.make_async_copy(source.at[cut], target.at[cut], sems.at[used]))
            used += 1
        copies.append(group)
    for group in copies:
        for copy in group:
            copy.start()
    return copies


def wait_all(group):
    for copy in group:
        copy.wait()


def project_rows(raw, ln, wk, wv, wq, qg, kg, cosine, sine, waits, q, k, v, pairs, at):
    gain = ln[...].astype(jnp.float32)
    rows = normalized(raw[...].astype(jnp.float32), gain).astype(jnp.bfloat16)
    wait_all(waits[0])
    turned_heads(dot(rows, wk[...]), kg, cosine, sine, k, at)
    wait_all(waits[1])
    v[at, :] = dot(rows, wv[...]).astype(jnp.bfloat16)
    pairs[...] = joined_heads(k[at, :], v[at, :])
    wait_all(waits[2])
    turned_heads(dot(rows, wq[...]), qg, cosine, sine, q, at)


def first_kernel(pieces, place, ids, *refs):
    rows_far = refs[: 1 + pieces]
    ln, wq_far, wk_far, wv_far, qg, kg, cos, sin = refs[1 + pieces : 9 + pieces]
    q, k, v, pairs, raw, wq, wk, wv, cos_rows, sin_rows, sems = refs[9 + pieces :]
    req, side, core = place[0], place[1], place[2]
    half = raw.shape[0]
    count = half // 2
    here = pl.ds(pl.multiple_of(side * half, half), half)
    moves = []
    at = core * count
    for i, far in enumerate(rows_far):
        step = far.shape[0]
        moves.append((far, raw.at[pl.ds(pl.multiple_of(at, step), step)], 1))
        at = at + step if i else (1 - core) * count
    moves += [
        (cos.at[here], cos_rows, 1),
        (sin.at[here], sin_rows, 1),
        (wk_far, wk, 1),
        (wv_far, wv, 1),
        (wq_far, wq, 1),
    ]
    copies = split_copies(moves, sems)
    for group in copies[:-3]:
        wait_all(group)
    cosine, sine, _ = angles(ids, req, side * half, cos_rows[...], sin_rows[...])
    project_rows(
        raw, ln, wk, wv, wq, qg, kg, cosine, sine, copies[-3:], q, k, v, pairs, slice(None)
    )


def first_half(place, ids, own, others, ln, wq, wk, wv, qg, kg, cos, sin):
    half, width = 2 * own.shape[0], own.shape[1]
    kv = wk.shape[1]
    bf = jnp.bfloat16
    return pl.pallas_call(
        functools.partial(first_kernel, len(others)),
        out_shape=[
            jax.ShapeDtypeStruct((half, wq.shape[1]), bf),
            jax.ShapeDtypeStruct((half, kv), bf),
            jax.ShapeDtypeStruct((half, kv), bf),
            jax.ShapeDtypeStruct((half, kv // HD, 2 * HD), bf),
        ],
        in_specs=[SMEM, VMEM]
        + [FAR] * (1 + len(others))
        + [VMEM, FAR, FAR, FAR, VMEM, VMEM, FAR, FAR],
        out_specs=[VMEM] * 4,
        scratch_shapes=[
            pltpu.VMEM((half, width), bf),
            pltpu.VMEM(wq.shape, bf),
            pltpu.VMEM(wk.shape, bf),
            pltpu.VMEM(wv.shape, bf),
            pltpu.VMEM((half, HD), jnp.float32),
            pltpu.VMEM((half, HD), jnp.float32),
            pltpu.SemaphoreType.DMA((6 + len(others),)),
        ],
        compiler_params=pltpu.CompilerParams(vmem_limit_bytes=MOST),
        cost_estimate=BRIEF,
        name="first_half",
    )(place, ids, own, *others, ln, wq, wk, wv, qg, kg, cos, sin)


def second_kernel(
    place, ids, mine_far, other_far, ln, wq_far, wk_far, wv_far, qg, kg, cos, sin,
    qa, ka, va, pairs, keep, send,
    raw, wq, wk, wv, cos_rows, sin_rows, q, k, v, mixed, sems,
):
    req, side, core = place[0], place[1], place[2]
    half = raw.shape[0]
    count = half // 2
    near = pl.ds(pl.multiple_of(side * half, half), half)
    far = pl.ds(pl.multiple_of((1 - side) * half, half), half)
    copies = split_copies(
        (
            (mine_far, raw.at[pl.ds(pl.multiple_of(core * count, count), count)], 1),
            (other_far, raw.at[pl.ds(pl.multiple_of((1 - core) * count, count), count)], 1),
            (cos.at[far], cos_rows, 1),
            (sin.at[far], sin_rows, 1),
            (wk_far, wk, 1),
            (wv_far, wv, 1),
            (wq_far, wq, 1),
            (ka, k.at[near], 1),
            (qa, q.at[near], 1),
            (va, v.at[near], 1),
        ),
        sems,
    )
    for group in copies[:4]:
        wait_all(group)
    cosine, sine, begins = angles(ids, req, (1 - side) * half, cos_rows[...], sin_rows[...])
    project_rows(
        raw, ln, wk, wv, wq, qg, kg, cosine, sine, copies[4:7], q, k, v, pairs, far
    )
    for group in copies[7:]:
        wait_all(group)
    kv_here = k.shape[1] // HD
    group = q.shape[1] // k.shape[1]
    scale = 1.0 / math.sqrt(HD)
    for block in range(2):
        seen = (block + 1) * half
        here = slice(block * half, seen)
        token = block * half + lax.broadcasted_iota(jnp.int32, (half, seen), 0)
        column = lax.broadcasted_iota(jnp.int32, (half, seen), 1)
        start = jnp.zeros_like(token)
        for begin in begins:
            start = jnp.where(token >= begin, begin, start)
        allowed = (column <= token) & (column >= start)
        for j in range(kv_here):
            lanes = slice(j * HD, (j + 1) * HD)
            heads = range(j * group, (j + 1) * group)
            scores = lax.dot_general(
                jnp.concatenate([q[here, h * HD : (h + 1) * HD] for h in heads], axis=0),
                k[:seen, lanes],
                (((1,), (1,)), ((), ())),
                preferred_element_type=jnp.float32,
            )
            raised = [
                jnp.where(allowed, jnp.exp(scores[i * half : (i + 1) * half] * scale), 0.0)
                for i in range(group)
            ]
            summed = dot(
                jnp.concatenate([r.astype(jnp.bfloat16) for r in raised], axis=0),
                v[:seen, lanes],
            )
            for i, h in enumerate(heads):
                share = 1.0 / jnp.sum(raised[i], axis=-1, keepdims=True)
                mixed[here, h * HD : (h + 1) * HD] = (
                    summed[i * half : (i + 1) * half] * share
                ).astype(jnp.bfloat16)
    mine = 2 * side + core
    for distance in range(4):
        out = send if distance % 2 else keep
        at = pl.ds(pl.multiple_of((mine ^ distance) * count, count), count)
        out[distance // 2 * count : (distance // 2 + 1) * count, :] = mixed[at, :]


def second_half(place, ids, mine, other, ln, wq, wk, wv, qg, kg, cos, sin, qa, ka, va):
    half, width = 2 * mine.shape[0], mine.shape[1]
    kv = wk.shape[1]
    bf = jnp.bfloat16
    return pl.pallas_call(
        second_kernel,
        out_shape=[jax.ShapeDtypeStruct((half, kv // HD, 2 * HD), bf)]
        + [jax.ShapeDtypeStruct((half, wq.shape[1]), bf)] * 2,
        in_specs=[SMEM, VMEM, FAR, FAR, VMEM, FAR, FAR, FAR, VMEM, VMEM] + [FAR] * 5,
        out_specs=[VMEM] * 3,
        scratch_shapes=[
            pltpu.VMEM((half, width), bf),
            pltpu.VMEM(wq.shape, bf),
            pltpu.VMEM(wk.shape, bf),
            pltpu.VMEM(wv.shape, bf),
            pltpu.VMEM((half, HD), jnp.float32),
            pltpu.VMEM((half, HD), jnp.float32),
            pltpu.VMEM((2 * half, wq.shape[1]), bf),
            pltpu.VMEM((2 * half, kv), bf),
            pltpu.VMEM((2 * half, kv), bf),
            pltpu.VMEM((2 * half, wq.shape[1]), bf),
            pltpu.SemaphoreType.DMA((10,)),
        ],
        compiler_params=pltpu.CompilerParams(vmem_limit_bytes=MOST),
        cost_estimate=BRIEF,
        name="second_half",
    )(place, ids, mine, other, ln, wq, wk, wv, qg, kg, cos, sin, qa, ka, va)


def mlp_kernel(pieces, *refs):
    ln, wg, wu, keep, send, normed = refs[pieces:]
    count = keep.shape[0]
    gain = ln[...].astype(jnp.float32)
    at = 0
    for ref in refs[:pieces]:
        normed[at : at + ref.shape[0], :] = normalized(
            ref[...].astype(jnp.float32), gain
        ).astype(jnp.bfloat16)
        at += ref.shape[0]
    rows = normed[...]
    step = 256
    for at in range(0, wg.shape[1], step):
        lanes = slice(at, at + step)
        gate = dot(rows, wg[:, lanes])
        upper = dot(rows, wu[:, lanes])
        hidden = (gate / (1.0 + jnp.exp(-gate)) * upper).astype(jnp.bfloat16)
        keep[:, lanes] = hidden[:count]
        send[:, lanes] = hidden[count:]


def mlp(first, others, ln, wg, wu):
    count, width = first.shape
    out = jax.ShapeDtypeStruct((count, wg.shape[1]), jnp.bfloat16)
    return pl.pallas_call(
        functools.partial(mlp_kernel, 1 + len(others)),
        out_shape=[out] * 2,
        in_specs=[VMEM] * (4 + len(others)),
        out_specs=[VMEM] * 2,
        scratch_shapes=[pltpu.VMEM((2 * count, width), jnp.bfloat16)],
        compiler_params=pltpu.CompilerParams(vmem_limit_bytes=24 << 20),
        cost_estimate=BRIEF,
        name="gate_up",
    )(first, *others, ln, wg, wu)


class Part:
    def __init__(self, packed, base):
        self.packed, self.base = packed, base

    def __getitem__(self, i):
        return self.packed[self.base + i]


def page_kernel(rows, requests, entries, blocks, *refs):
    homes, packed = refs[:2]
    arrived = refs[2 : 2 + blocks]
    out, held, blank, where, load_sems, sems = refs[-6:]
    bounds = Part(packed, 0)
    prompts = Part(packed, (PROMPTS_DEV + 1) * where.shape[0])
    table = Part(packed, prompts.base + requests)
    half = rows // 2
    side = homes[blocks // 2]
    loads = [
        pltpu.make_async_copy(
            ref,
            held.at[pl.ds(pl.multiple_of(i // 2 * rows + (side ^ (i % 2)) * half, half), half)],
            load_sems.at[i],
        )
        for i, ref in enumerate(arrived)
    ]
    for load in loads:
        load.start()
    blank[...] = jnp.zeros_like(blank)

    def forget(g, carry):
        where[g] = -1
        return carry

    lax.fori_loop(0, where.shape[0], forget, 0)
    for i in range(blocks // 2):
        where[homes[i]] = i

    def taken(r):
        return where[prompts[r] // PROMPTS_DEV] >= 0

    def span(r):
        prompt = prompts[r]
        g = prompt // PROMPTS_DEV
        slot = g * (PROMPTS_DEV + 1) + prompt - g * PROMPTS_DEV
        begin = bounds[slot]
        return where[g] * rows + begin, bounds[slot + 1] - begin

    def clear(r, carry):
        def clear_page(e, c):
            pltpu.make_async_copy(blank, out.at[table[r * entries + e]], sems.at[r]).start()
            return c

        @pl.when(taken(r))
        def _():
            lax.fori_loop((span(r)[1] + PAGE - 1) // PAGE, entries, clear_page, 0)

        return carry

    lax.fori_loop(0, requests, clear, 0)
    for load in loads:
        load.wait()

    def pieces(amount, first, start):
        for size in (8, 4, 2, 1):
            skipped = amount - amount % (2 * size)

            @pl.when((amount // size) % 2 == 1)
            def _():
                start(first + skipped, size)

    def issue(r, carry):
        @pl.when(taken(r))
        def _():
            issue_one(r)

        return carry

    def issue_one(r):
        begin, length = span(r)
        full = length // PAGE
        rest = length - full * PAGE

        def copy_page(e, c):
            pltpu.make_async_copy(
                held.at[pl.ds(begin + e * PAGE, PAGE)], out.at[table[r * entries + e]], sems.at[r]
            ).start()
            return c

        lax.fori_loop(0, full, copy_page, 0)

        @pl.when(rest > 0)
        def _():
            page = table[r * entries + full]
            base = begin + full * PAGE

            def kept(at, size):
                pltpu.make_async_copy(
                    held.at[pl.ds(base + at, size)], out.at[page, pl.ds(at, size)], sems.at[r]
                ).start()

            def blanked(at, size):
                pltpu.make_async_copy(
                    blank.at[pl.ds(0, size)], out.at[page, pl.ds(at, size)], sems.at[r]
                ).start()

            pieces(rest, 0, kept)
            pieces(PAGE - rest, rest, blanked)

    lax.fori_loop(0, requests, issue, 0)

    def finish(r, carry):
        @pl.when(taken(r))
        def _():
            pltpu.make_async_copy(
                out.at[pl.ds(0, entries)], out.at[pl.ds(0, entries)], sems.at[r]
            ).wait()

        return carry

    lax.fori_loop(0, requests, finish, 0)


def fill_pages(packed, requests, entries, arrived, homes, rows, cache=None):
    bounds = packed.shape[0] - requests * (1 + entries)
    row_shape, dtype = arrived[0].shape[1:], arrived[0].dtype
    blocks = len(arrived)
    given = [] if cache is None else [cache]
    held = (blocks // 2 * rows,) + row_shape
    return pl.pallas_call(
        functools.partial(page_kernel, rows, requests, entries, blocks),
        out_shape=jax.ShapeDtypeStruct((requests * entries, PAGE) + row_shape, dtype),
        in_specs=[SMEM] * 2 + [FAR] * blocks + [ANY] * len(given),
        out_specs=ANY,
        scratch_shapes=[
            pltpu.VMEM(held, dtype),
            pltpu.VMEM((PAGE,) + row_shape, dtype),
            pltpu.SMEM((bounds // (PROMPTS_DEV + 1),), jnp.int32),
            pltpu.SemaphoreType.DMA((blocks,)),
            pltpu.SemaphoreType.DMA((requests,)),
        ],
        input_output_aliases={2 + blocks: 0} if given else {},
        compiler_params=pltpu.CompilerParams(vmem_limit_bytes=MOST),
        cost_estimate=BRIEF,
        name="fill_pages",
    )(homes, packed, *arrived, *given)


def body(
    hidden_in,
    segment_ids,
    request_prompt,
    page_table,
    ln_attn,
    w_query,
    w_key,
    w_value,
    q_gain,
    k_gain,
    w_out,
    ln_mlp,
    w_gate,
    w_up,
    w_down,
):
    parts = lax.axis_size("mp")
    groups = lax.axis_size("req")
    rows = hidden_in.shape[0] * parts
    half = rows // 2
    req = lax.axis_index("req")
    mine = lax.axis_index("mp")
    side, core = mine // 2, mine % 2
    to_core = [(i, i ^ 1) for i in range(parts)]
    to_side = [(i, i ^ 2) for i in range(parts)]
    to_pair = [(i, i ^ 1) for i in range(groups)]
    to_next = [(i, (i + 2) % groups) for i in range(groups)]

    def by_core(a):
        return lax.ppermute(a, "mp", to_core)

    def by_core_in_pieces(a):
        return [by_core(piece) for piece in jnp.split(a, 2)]

    def by_side(a):
        return lax.ppermute(a, "mp", to_side)

    def forward(a):
        return lax.ppermute(a, "req", to_next)

    def flipped(a):
        return lax.ppermute(a, "req", to_pair)

    here_x = by_side(hidden_in)
    here_c = by_core_in_pieces(hidden_in)
    steps = groups // 2
    homes = [(req - 2 * step) % groups for step in range(steps)]
    homes += [((req ^ 1) - 2 * step) % groups for step in range(steps)]
    place = jnp.stack([req, side, core]).astype(jnp.int32)
    ln = ln_attn.reshape(1, -1)
    qg, kg = q_gain.reshape(1, -1), k_gain.reshape(1, -1)
    cos, sin = turns(rows)
    tables = (ln, w_query, w_key, w_value, qg, kg, cos, sin)
    qa, ka, va, pairs_a = first_half(place, segment_ids, hidden_in, here_c, *tables)
    line_a, flips_a = [pairs_a, forward(pairs_a)], [flipped(pairs_a)]
    bounds = segment_bounds(ordered(segment_ids, ka))
    out_other = by_core(w_out)
    first_homes = jnp.stack(homes[: steps - 1] + homes[steps : 2 * steps - 2] + [side])
    last_homes = jnp.stack([homes[steps - 1], homes[-2], homes[-1], side])
    requests, entries = page_table.shape
    packed = jnp.concatenate([bounds, request_prompt, page_table.reshape(-1)])
    here_x, packed, first_homes, last_homes = lax.optimization_barrier(
        (here_x, packed, first_homes.astype(jnp.int32), last_homes.astype(jnp.int32))
    )
    here_x = ordered(here_x, out_other)
    here_xc = by_core(here_x)
    down_other = by_core(ordered(w_down, here_xc))
    pairs_b, keep, send = second_half(
        place, segment_ids, here_x, here_xc, *tables, qa, ka, va
    )
    send = ordered(ordered(send, line_a[1]), flips_a[0])
    got = by_core(send)
    part_b = (dot(keep[half // 2 :], w_out) + dot(got[half // 2 :], out_other)).astype(
        jnp.bfloat16
    )
    part_b = ordered(part_b, down_other)
    back = by_side(part_b)
    keep, got = ordered(keep, part_b), ordered(got, part_b)
    part_a = dot(keep[: half // 2], w_out) + dot(got[: half // 2], out_other)
    back = ordered(back, part_a)
    after = (hidden_in.astype(jnp.float32) + part_a + back.astype(jnp.float32)).astype(
        jnp.bfloat16
    )


    def advance(line, flips):
        flips.append(flipped(line[-1]))
        line.append(forward(line[-1]))

    line_b, flips_b = [pairs_b], []
    line_a[1], line_b[0] = ordered(line_a[1], part_b), ordered(line_b[0], part_b)
    advance(line_a, flips_a)
    advance(line_b, flips_b)
    after = ordered(after, line_a[-1], line_b[-1], flips_a[-1], flips_b[-1])
    after_x = by_side(after)
    after_c = [by_core(after)]
    ln2 = ln_mlp.reshape(1, -1)
    line_a[-1], line_b[-1] = ordered((line_a[-1], line_b[-1]), after)
    advance(line_a, flips_a)
    advance(line_b, flips_b)
    keep_a, send_a = mlp(after, after_c, ln2, w_gate, w_up)
    after_x = ordered(after_x, keep_a)
    for arrival in (line_b[-1], line_a[-1], flips_b[-1], flips_a[-1]):
        after_x = ordered(after_x, arrival)
    after_xc = by_core(after_x)
    got_a = by_core(send_a)
    down_a = dot(keep_a, w_down) + dot(got_a, down_other)
    after_xc = ordered(after_xc, down_a)
    keep_b, send_b = mlp(after_x, [after_xc], ln2, w_gate, w_up)
    line_a[-1], line_b[-1], flips_a[-1] = ordered(
        (line_a[-1], line_b[-1], flips_a[-1]), after_x
    )
    for step in range(4, steps):
        advance(line_a, flips_a)
        advance(line_b, flips_b)
    flips_a.append(forward(flips_a[-1]))
    advance(line_b, flips_b)
    got_b = by_core(send_b)
    down_b = (dot(keep_b, w_down) + dot(got_b, down_other)).astype(jnp.bfloat16)
    back = by_side(down_b)
    tables = (ordered(packed, down_b, line_b[-1]), requests, entries)
    blocks = list(zip(line_a, line_b))[: steps - 1] + list(zip(flips_a, flips_b))[: steps - 2]
    cache = fill_pages(
        *tables,
        [part for block in blocks for part in block],
        first_homes,
        rows,
    )
    flips_b.append(flipped(ordered(line_b[-1], flips_b[-1])))
    cache = fill_pages(
        *tables,
        [line_a[-1], line_b[-1], flips_a[-2], flips_b[-2], flips_a[-1], flips_b[-1]],
        last_homes,
        rows,
        cache,
    )
    result = (after.astype(jnp.float32) + down_a + back.astype(jnp.float32)).astype(jnp.bfloat16)
    return (result, cache)


def solution(mesh):
    return jax.shard_map(
        body,
        mesh=mesh,
        in_specs=(
            P(("req", "mp"), None),
            P(),
            P("req"),
            P("req", None),
            P(),
            P(None, "mp"),
            P(None, "mp"),
            P(None, "mp"),
            P(),
            P(),
            P("mp", None),
            P(),
            P(None, "mp"),
            P(None, "mp"),
            P("mp", None),
        ),
        out_specs=(P(("req", "mp"), None), P("req", None, "mp", None)),
        check_vma=False,
    )
```

```python
import functools
import math

import jax
import jax.numpy as jnp
import numpy as np
from jax import lax
from jax.experimental import pallas as pl
from jax.experimental.pallas import tpu as pltpu
from jax.sharding import PartitionSpec as P

HD = 128
PROMPTS_DEV = 3
PAGE = 16
EPS = 1e-06
THETA = 1000000.0
SMEM = pl.BlockSpec(memory_space=pltpu.SMEM)
VMEM = pl.BlockSpec(memory_space=pltpu.VMEM)
ANY = pl.BlockSpec(memory_space=pl.ANY)
FAR = pl.BlockSpec(memory_space=pltpu.HBM)
MOST = 61 * 10**6
BRIEF = pl.CostEstimate(flops=1, bytes_accessed=1, transcendentals=0)


def dot(a, b):
    return jnp.dot(a, b, preferred_element_type=jnp.float32)


def ordered(value, *earlier):
    return lax.optimization_barrier((value,) + earlier)[0]


def normalized(wide, gain):
    return wide * lax.rsqrt(jnp.mean(wide * wide, axis=-1, keepdims=True) + EPS) * gain


def segment_bounds(segment_ids):
    limits = jnp.arange(PROMPTS_DEV + 1, dtype=jnp.int32)
    below = segment_ids[:, None, :] < limits[None, :, None]
    return jnp.sum(below.astype(jnp.int32), axis=2).reshape(-1)


def turns(rows):
    freq = THETA ** (-(np.arange(HD // 2) * 2.0) / HD)
    angle = np.arange(rows)[:, None] * np.concatenate([freq, freq])[None, :]
    return np.cos(angle).astype(np.float32), np.sin(angle).astype(np.float32)


def angles(ids, req, first, cos_rows, sin_rows):
    row = ids[pl.ds(req, 1), :]
    begins = [jnp.sum((row < s).astype(jnp.int32)) for s in range(1, PROMPTS_DEV)]
    line = lax.broadcasted_iota(jnp.int32, (8, HD), 0)
    lane = lax.broadcasted_iota(jnp.int32, (8, HD), 1)
    turn = jnp.where(lane < HD // 2, lane, lane - HD // 2).astype(jnp.float32)
    back = jnp.zeros((8, HD), jnp.float32)
    for s, begin in enumerate(begins):
        back = jnp.where(line == s + 1, begin.astype(jnp.float32), back)
    back = back * jnp.exp(turn * (-2.0 / HD * math.log(THETA)))
    back_cos, back_sin = jnp.cos(back), jnp.sin(back)
    token = first + lax.broadcasted_iota(jnp.int32, cos_rows.shape, 0)
    less_cos, less_sin = back_cos[0:1, :], back_sin[0:1, :]
    for s, begin in enumerate(begins):
        later = token >= begin
        less_cos = jnp.where(later, back_cos[s + 1 : s + 2, :], less_cos)
        less_sin = jnp.where(later, back_sin[s + 1 : s + 2, :], less_sin)
    cosine = cos_rows * less_cos + sin_rows * less_sin
    sine = sin_rows * less_cos - cos_rows * less_sin
    first_half = lax.broadcasted_iota(jnp.int32, cos_rows.shape, 1) < HD // 2
    return cosine, jnp.where(first_half, -sine, sine), begins


def turned_heads(wide, gain_ref, cosine, sine, out, at):
    gain = gain_ref[...].astype(jnp.float32)
    for h in range(wide.shape[1] // HD):
        one = normalized(wide[:, h * HD : (h + 1) * HD], gain)
        turned = one * cosine + pltpu.roll(one, HD // 2, 1) * sine
        out[at, h * HD : (h + 1) * HD] = turned.astype(jnp.bfloat16)


def joined_heads(k, v):
    shape = (k.shape[0], k.shape[1] // HD, HD)
    return jnp.concatenate([k.reshape(shape), v.reshape(shape)], axis=-1)


def split_copies(moves, sems):
    copies, used = [], 0
    for source, target, parts in moves:
        step = source.shape[0] // parts
        group = []
        for i in range(parts):
            cut = pl.ds(i * step, step)
            group.append(pltpu.make_async_copy(source.at[cut], target.at[cut], sems.at[used]))
            used += 1
        copies.append(group)
    for group in copies:
        for copy in group:
            copy.start()
    return copies


def wait_all(group):
    for copy in group:
        copy.wait()


def project_rows(raw, ln, wk, wv, wq, qg, kg, cosine, sine, waits, q, k, v, pairs, at):
    gain = ln[...].astype(jnp.float32)
    rows = normalized(raw[...].astype(jnp.float32), gain).astype(jnp.bfloat16)
    wait_all(waits[0])
    turned_heads(dot(rows, wk[...]), kg, cosine, sine, k, at)
    wait_all(waits[1])
    v[at, :] = dot(rows, wv[...]).astype(jnp.bfloat16)
    pairs[...] = joined_heads(k[at, :], v[at, :])
    wait_all(waits[2])
    turned_heads(dot(rows, wq[...]), qg, cosine, sine, q, at)


def first_kernel(pieces, place, ids, *refs):
    rows_far = refs[: 1 + pieces]
    ln, wq_far, wk_far, wv_far, qg, kg, cos, sin = refs[1 + pieces : 9 + pieces]
    q, k, v, pairs, raw, wq, wk, wv, cos_rows, sin_rows, sems = refs[9 + pieces :]
    req, side, core = place[0], place[1], place[2]
    half = raw.shape[0]
    count = half // 2
    here = pl.ds(pl.multiple_of(side * half, half), half)
    moves = []
    at = core * count
    for i, far in enumerate(rows_far):
        step = far.shape[0]
        moves.append((far, raw.at[pl.ds(pl.multiple_of(at, step), step)], 1))
        at = at + step if i else (1 - core) * count
    moves += [
        (cos.at[here], cos_rows, 1),
        (sin.at[here], sin_rows, 1),
        (wk_far, wk, 1),
        (wv_far, wv, 1),
        (wq_far, wq, 1),
    ]
    copies = split_copies(moves, sems)
    for group in copies[:-3]:
        wait_all(group)
    cosine, sine, _ = angles(ids, req, side * half, cos_rows[...], sin_rows[...])
    project_rows(
        raw, ln, wk, wv, wq, qg, kg, cosine, sine, copies[-3:], q, k, v, pairs, slice(None)
    )


def first_half(place, ids, own, others, ln, wq, wk, wv, qg, kg, cos, sin):
    half, width = 2 * own.shape[0], own.shape[1]
    kv = wk.shape[1]
    bf = jnp.bfloat16
    return pl.pallas_call(
        functools.partial(first_kernel, len(others)),
        out_shape=[
            jax.ShapeDtypeStruct((half, wq.shape[1]), bf),
            jax.ShapeDtypeStruct((half, kv), bf),
            jax.ShapeDtypeStruct((half, kv), bf),
            jax.ShapeDtypeStruct((half, kv // HD, 2 * HD), bf),
        ],
        in_specs=[SMEM, VMEM]
        + [FAR] * (1 + len(others))
        + [VMEM, FAR, FAR, FAR, VMEM, VMEM, FAR, FAR],
        out_specs=[VMEM] * 4,
        scratch_shapes=[
            pltpu.VMEM((half, width), bf),
            pltpu.VMEM(wq.shape, bf),
            pltpu.VMEM(wk.shape, bf),
            pltpu.VMEM(wv.shape, bf),
            pltpu.VMEM((half, HD), jnp.float32),
            pltpu.VMEM((half, HD), jnp.float32),
            pltpu.SemaphoreType.DMA((6 + len(others),)),
        ],
        compiler_params=pltpu.CompilerParams(vmem_limit_bytes=MOST),
        cost_estimate=BRIEF,
        name="first_half",
    )(place, ids, own, *others, ln, wq, wk, wv, qg, kg, cos, sin)


def second_kernel(
    place, ids, mine_far, other_far, ln, wq_far, wk_far, wv_far, qg, kg, cos, sin,
    qa, ka, va, pairs, keep, send,
    raw, wq, wk, wv, cos_rows, sin_rows, q, k, v, mixed, sems,
):
    req, side, core = place[0], place[1], place[2]
    half = raw.shape[0]
    count = half // 2
    near = pl.ds(pl.multiple_of(side * half, half), half)
    far = pl.ds(pl.multiple_of((1 - side) * half, half), half)
    copies = split_copies(
        (
            (mine_far, raw.at[pl.ds(pl.multiple_of(core * count, count), count)], 1),
            (other_far, raw.at[pl.ds(pl.multiple_of((1 - core) * count, count), count)], 1),
            (cos.at[far], cos_rows, 1),
            (sin.at[far], sin_rows, 1),
            (wk_far, wk, 1),
            (wv_far, wv, 1),
            (wq_far, wq, 1),
            (ka, k.at[near], 1),
            (qa, q.at[near], 1),
            (va, v.at[near], 1),
        ),
        sems,
    )
    for group in copies[:4]:
        wait_all(group)
    cosine, sine, begins = angles(ids, req, (1 - side) * half, cos_rows[...], sin_rows[...])
    project_rows(
        raw, ln, wk, wv, wq, qg, kg, cosine, sine, copies[4:7], q, k, v, pairs, far
    )
    for group in copies[7:]:
        wait_all(group)
    kv_here = k.shape[1] // HD
    group = q.shape[1] // k.shape[1]
    scale = 1.0 / math.sqrt(HD)
    for block in range(2):
        seen = (block + 1) * half
        here = slice(block * half, seen)
        token = block * half + lax.broadcasted_iota(jnp.int32, (half, seen), 0)
        column = lax.broadcasted_iota(jnp.int32, (half, seen), 1)
        start = jnp.zeros_like(token)
        for begin in begins:
            start = jnp.where(token >= begin, begin, start)
        allowed = (column <= token) & (column >= start)
        for j in range(kv_here):
            lanes = slice(j * HD, (j + 1) * HD)
            heads = range(j * group, (j + 1) * group)
            scores = lax.dot_general(
                jnp.concatenate([q[here, h * HD : (h + 1) * HD] for h in heads], axis=0),
                k[:seen, lanes],
                (((1,), (1,)), ((), ())),
                preferred_element_type=jnp.float32,
            )
            raised = [
                jnp.where(allowed, jnp.exp(scores[i * half : (i + 1) * half] * scale), 0.0)
                for i in range(group)
            ]
            summed = dot(
                jnp.concatenate([r.astype(jnp.bfloat16) for r in raised], axis=0),
                v[:seen, lanes],
            )
            for i, h in enumerate(heads):
                share = 1.0 / jnp.sum(raised[i], axis=-1, keepdims=True)
                mixed[here, h * HD : (h + 1) * HD] = (
                    summed[i * half : (i + 1) * half] * share
                ).astype(jnp.bfloat16)
    mine = 2 * side + core
    for distance in range(4):
        out = send if distance % 2 else keep
        at = pl.ds(pl.multiple_of((mine ^ distance) * count, count), count)
        out[distance // 2 * count : (distance // 2 + 1) * count, :] = mixed[at, :]


def second_half(place, ids, mine, other, ln, wq, wk, wv, qg, kg, cos, sin, qa, ka, va):
    half, width = 2 * mine.shape[0], mine.shape[1]
    kv = wk.shape[1]
    bf = jnp.bfloat16
    return pl.pallas_call(
        second_kernel,
        out_shape=[jax.ShapeDtypeStruct((half, kv // HD, 2 * HD), bf)]
        + [jax.ShapeDtypeStruct((half, wq.shape[1]), bf)] * 2,
        in_specs=[SMEM, VMEM, FAR, FAR, VMEM, FAR, FAR, FAR, VMEM, VMEM] + [FAR] * 5,
        out_specs=[VMEM] * 3,
        scratch_shapes=[
            pltpu.VMEM((half, width), bf),
            pltpu.VMEM(wq.shape, bf),
            pltpu.VMEM(wk.shape, bf),
            pltpu.VMEM(wv.shape, bf),
            pltpu.VMEM((half, HD), jnp.float32),
            pltpu.VMEM((half, HD), jnp.float32),
            pltpu.VMEM((2 * half, wq.shape[1]), bf),
            pltpu.VMEM((2 * half, kv), bf),
            pltpu.VMEM((2 * half, kv), bf),
            pltpu.VMEM((2 * half, wq.shape[1]), bf),
            pltpu.SemaphoreType.DMA((10,)),
        ],
        compiler_params=pltpu.CompilerParams(vmem_limit_bytes=MOST),
        cost_estimate=BRIEF,
        name="second_half",
    )(place, ids, mine, other, ln, wq, wk, wv, qg, kg, cos, sin, qa, ka, va)


def mlp_kernel(pieces, *refs):
    ln, wg, wu, keep, send, normed = refs[pieces:]
    count = keep.shape[0]
    gain = ln[...].astype(jnp.float32)
    at = 0
    for ref in refs[:pieces]:
        normed[at : at + ref.shape[0], :] = normalized(
            ref[...].astype(jnp.float32), gain
        ).astype(jnp.bfloat16)
        at += ref.shape[0]
    rows = normed[...]
    step = 256
    for at in range(0, wg.shape[1], step):
        lanes = slice(at, at + step)
        gate = dot(rows, wg[:, lanes])
        upper = dot(rows, wu[:, lanes])
        hidden = (gate / (1.0 + jnp.exp(-gate)) * upper).astype(jnp.bfloat16)
        keep[:, lanes] = hidden[:count]
        send[:, lanes] = hidden[count:]


def mlp(first, others, ln, wg, wu):
    count, width = first.shape
    out = jax.ShapeDtypeStruct((count, wg.shape[1]), jnp.bfloat16)
    return pl.pallas_call(
        functools.partial(mlp_kernel, 1 + len(others)),
        out_shape=[out] * 2,
        in_specs=[VMEM] * (4 + len(others)),
        out_specs=[VMEM] * 2,
        scratch_shapes=[pltpu.VMEM((2 * count, width), jnp.bfloat16)],
        compiler_params=pltpu.CompilerParams(vmem_limit_bytes=24 << 20),
        cost_estimate=BRIEF,
        name="gate_up",
    )(first, *others, ln, wg, wu)


class Part:
    def __init__(self, packed, base):
        self.packed, self.base = packed, base

    def __getitem__(self, i):
        return self.packed[self.base + i]


def page_kernel(rows, requests, entries, blocks, *refs):
    homes, packed = refs[:2]
    arrived = refs[2 : 2 + blocks]
    out, held, blank, where, load_sems, sems = refs[-6:]
    bounds = Part(packed, 0)
    prompts = Part(packed, (PROMPTS_DEV + 1) * where.shape[0])
    table = Part(packed, prompts.base + requests)
    half = rows // 2
    side = homes[blocks // 2]
    loads = [
        pltpu.make_async_copy(
            ref,
            held.at[pl.ds(pl.multiple_of(i // 2 * rows + (side ^ (i % 2)) * half, half), half)],
            load_sems.at[i],
        )
        for i, ref in enumerate(arrived)
    ]
    for load in loads:
        load.start()
    blank[...] = jnp.zeros_like(blank)

    def forget(g, carry):
        where[g] = -1
        return carry

    lax.fori_loop(0, where.shape[0], forget, 0)
    for i in range(blocks // 2):
        where[homes[i]] = i

    def taken(r):
        return where[prompts[r] // PROMPTS_DEV] >= 0

    def span(r):
        prompt = prompts[r]
        g = prompt // PROMPTS_DEV
        slot = g * (PROMPTS_DEV + 1) + prompt - g * PROMPTS_DEV
        begin = bounds[slot]
        return where[g] * rows + begin, bounds[slot + 1] - begin

    def clear(r, carry):
        def clear_page(e, c):
            pltpu.make_async_copy(blank, out.at[table[r * entries + e]], sems.at[r]).start()
            return c

        @pl.when(taken(r))
        def _():
            lax.fori_loop((span(r)[1] + PAGE - 1) // PAGE, entries, clear_page, 0)

        return carry

    lax.fori_loop(0, requests, clear, 0)
    for load in loads:
        load.wait()

    def pieces(amount, first, start):
        for size in (8, 4, 2, 1):
            skipped = amount - amount % (2 * size)

            @pl.when((amount // size) % 2 == 1)
            def _():
                start(first + skipped, size)

    def issue(r, carry):
        @pl.when(taken(r))
        def _():
            issue_one(r)

        return carry

    def issue_one(r):
        begin, length = span(r)
        full = length // PAGE
        rest = length - full * PAGE

        def copy_page(e, c):
            pltpu.make_async_copy(
                held.at[pl.ds(begin + e * PAGE, PAGE)], out.at[table[r * entries + e]], sems.at[r]
            ).start()
            return c

        lax.fori_loop(0, full, copy_page, 0)

        @pl.when(rest > 0)
        def _():
            page = table[r * entries + full]
            base = begin + full * PAGE

            def kept(at, size):
                pltpu.make_async_copy(
                    held.at[pl.ds(base + at, size)], out.at[page, pl.ds(at, size)], sems.at[r]
                ).start()

            def blanked(at, size):
                pltpu.make_async_copy(
                    blank.at[pl.ds(0, size)], out.at[page, pl.ds(at, size)], sems.at[r]
                ).start()

            pieces(rest, 0, kept)
            pieces(PAGE - rest, rest, blanked)

    lax.fori_loop(0, requests, issue, 0)

    def finish(r, carry):
        @pl.when(taken(r))
        def _():
            pltpu.make_async_copy(
                out.at[pl.ds(0, entries)], out.at[pl.ds(0, entries)], sems.at[r]
            ).wait()

        return carry

    lax.fori_loop(0, requests, finish, 0)


def fill_pages(packed, requests, entries, arrived, homes, rows, cache=None):
    bounds = packed.shape[0] - requests * (1 + entries)
    row_shape, dtype = arrived[0].shape[1:], arrived[0].dtype
    blocks = len(arrived)
    given = [] if cache is None else [cache]
    held = (blocks // 2 * rows,) + row_shape
    return pl.pallas_call(
        functools.partial(page_kernel, rows, requests, entries, blocks),
        out_shape=jax.ShapeDtypeStruct((requests * entries, PAGE) + row_shape, dtype),
        in_specs=[SMEM] * 2 + [FAR] * blocks + [ANY] * len(given),
        out_specs=ANY,
        scratch_shapes=[
            pltpu.VMEM(held, dtype),
            pltpu.VMEM((PAGE,) + row_shape, dtype),
            pltpu.SMEM((bounds // (PROMPTS_DEV + 1),), jnp.int32),
            pltpu.SemaphoreType.DMA((blocks,)),
            pltpu.SemaphoreType.DMA((requests,)),
        ],
        input_output_aliases={2 + blocks: 0} if given else {},
        compiler_params=pltpu.CompilerParams(vmem_limit_bytes=MOST),
        cost_estimate=BRIEF,
        name="fill_pages",
    )(homes, packed, *arrived, *given)


def body(
    hidden_in,
    segment_ids,
    request_prompt,
    page_table,
    ln_attn,
    w_query,
    w_key,
    w_value,
    q_gain,
    k_gain,
    w_out,
    ln_mlp,
    w_gate,
    w_up,
    w_down,
):
    parts = lax.axis_size("mp")
    groups = lax.axis_size("req")
    rows = hidden_in.shape[0] * parts
    half = rows // 2
    req = lax.axis_index("req")
    mine = lax.axis_index("mp")
    side, core = mine // 2, mine % 2
    to_core = [(i, i ^ 1) for i in range(parts)]
    to_side = [(i, i ^ 2) for i in range(parts)]
    to_pair = [(i, i ^ 1) for i in range(groups)]
    to_next = [(i, (i + 2) % groups) for i in range(groups)]

    def by_core(a):
        return lax.ppermute(a, "mp", to_core)

    def by_core_in_pieces(a):
        return [by_core(piece) for piece in jnp.split(a, 2)]

    def by_side(a):
        return lax.ppermute(a, "mp", to_side)

    def forward(a):
        return lax.ppermute(a, "req", to_next)

    def flipped(a):
        return lax.ppermute(a, "req", to_pair)

    here_x = by_side(hidden_in)
    here_c = by_core_in_pieces(hidden_in)
    steps = groups // 2
    homes = [(req - 2 * step) % groups for step in range(steps)]
    homes += [((req ^ 1) - 2 * step) % groups for step in range(steps)]
    place = jnp.stack([req, side, core]).astype(jnp.int32)
    ln = ln_attn.reshape(1, -1)
    qg, kg = q_gain.reshape(1, -1), k_gain.reshape(1, -1)
    cos, sin = turns(rows)
    tables = (ln, w_query, w_key, w_value, qg, kg, cos, sin)
    qa, ka, va, pairs_a = first_half(place, segment_ids, hidden_in, here_c, *tables)
    line_a, flips_a = [pairs_a, forward(pairs_a)], [flipped(pairs_a)]
    bounds = segment_bounds(ordered(segment_ids, ka))
    out_other = by_core(w_out)
    first_homes = jnp.stack(homes[: steps - 1] + homes[steps : 2 * steps - 2] + [side])
    last_homes = jnp.stack([homes[steps - 1], homes[-2], homes[-1], side])
    requests, entries = page_table.shape
    packed = jnp.concatenate([bounds, request_prompt, page_table.reshape(-1)])
    here_x, packed, first_homes, last_homes = lax.optimization_barrier(
        (here_x, packed, first_homes.astype(jnp.int32), last_homes.astype(jnp.int32))
    )
    here_x = ordered(here_x, out_other)
    here_xc = by_core(here_x)
    down_other = by_core(ordered(w_down, here_xc))
    pairs_b, keep, send = second_half(
        place, segment_ids, here_x, here_xc, *tables, qa, ka, va
    )
    send = ordered(ordered(send, line_a[1]), flips_a[0])
    got = by_core(send)
    part_b = (dot(keep[half // 2 :], w_out) + dot(got[half // 2 :], out_other)).astype(
        jnp.bfloat16
    )
    part_b = ordered(part_b, down_other)
    back = by_side(part_b)
    keep, got = ordered(keep, part_b), ordered(got, part_b)
    part_a = dot(keep[: half // 2], w_out) + dot(got[: half // 2], out_other)
    back = ordered(back, part_a)
    after = (hidden_in.astype(jnp.float32) + part_a + back.astype(jnp.float32)).astype(
        jnp.bfloat16
    )


    def advance(line, flips):
        flips.append(flipped(line[-1]))
        line.append(forward(line[-1]))

    line_b, flips_b = [pairs_b], []
    line_a[1], line_b[0] = ordered(line_a[1], part_b), ordered(line_b[0], part_b)
    advance(line_a, flips_a)
    advance(line_b, flips_b)
    after = ordered(after, line_a[-1], line_b[-1], flips_a[-1], flips_b[-1])
    after_x = by_side(after)
    after_c = [by_core(after)]
    ln2 = ln_mlp.reshape(1, -1)
    line_a[-1], line_b[-1] = ordered((line_a[-1], line_b[-1]), after)
    advance(line_a, flips_a)
    advance(line_b, flips_b)
    keep_a, send_a = mlp(after, after_c, ln2, w_gate, w_up)
    after_x = ordered(after_x, keep_a)
    for arrival in (line_b[-1], line_a[-1], flips_b[-1], flips_a[-1]):
        after_x = ordered(after_x, arrival)
    after_xc = by_core(after_x)
    got_a = by_core(send_a)
    down_a = dot(keep_a, w_down) + dot(got_a, down_other)
    after_xc = ordered(after_xc, down_a)
    keep_b, send_b = mlp(after_x, [after_xc], ln2, w_gate, w_up)
    line_a[-1], line_b[-1], flips_a[-1] = ordered(
        (line_a[-1], line_b[-1], flips_a[-1]), after_x
    )
    for step in range(4, steps):
        advance(line_a, flips_a)
        advance(line_b, flips_b)
    flips_a.append(forward(flips_a[-1]))
    advance(line_b, flips_b)
    got_b = by_core(send_b)
    down_b = (dot(keep_b, w_down) + dot(got_b, down_other)).astype(jnp.bfloat16)
    back = by_side(down_b)
    tables = (ordered(packed, down_b, line_b[-1]), requests, entries)
    blocks = list(zip(line_a, line_b))[: steps - 1] + list(zip(flips_a, flips_b))[: steps - 2]
    cache = fill_pages(
        *tables,
        [part for block in blocks for part in block],
        first_homes,
        rows,
    )
    flips_b.append(flipped(ordered(line_b[-1], flips_b[-1])))
    cache = fill_pages(
        *tables,
        [line_a[-1], line_b[-1], flips_a[-2], flips_b[-2], flips_a[-1], flips_b[-1]],
        last_homes,
        rows,
        cache,
    )
    result = (after.astype(jnp.float32) + down_a + back.astype(jnp.float32)).astype(jnp.bfloat16)
    return (result, cache)


def solution(mesh):
    return jax.shard_map(
        body,
        mesh=mesh,
        in_specs=(
            P(("req", "mp"), None),
            P(),
            P("req"),
            P("req", None),
            P(),
            P(None, "mp"),
            P(None, "mp"),
            P(None, "mp"),
            P(),
            P(),
            P("mp", None),
            P(),
            P(None, "mp"),
            P(None, "mp"),
            P("mp", None),
        ),
        out_specs=(P(("req", "mp"), None), P("req", None, "mp", None)),
        check_vma=False,
    )
```
